512 devices in a mesh: grp: 16 (over z, y_lo), blk: 32 (over x, y_hi, core).
Axes of the slice: x: 4, y: 8 (y_hi: 4, y_lo: 2; y = y_hi * 2 + y_lo), z: 8, core: 2. Of those that a mesh axis runs over, the one named last changes fastest.
Arguments:
- activations: bfloat16 [16384, 16384], P('grp', 'blk'), may hold values from -8 to 8
- output_grads: bfloat16 [16384, 4096], P('blk', 'grp'), may hold values from -8 to 8
- grad_weight: bfloat16 [16384, 4096], P('blk', 'grp'), may hold values from -96 to 96
Outputs:
- preconditioned: bfloat16 [16384, 4096], P('blk', 'grp')
The draws below stay inside these ranges and needn't reach their ends.
All inputs are finite; a program needn't handle non-finite values.
Results may differ from the reference program's by a relative error of at most 0.01.
The reference program's roundings to bfloat16 on the way count: a program that leaves them out, or rounds other values in their place, can miss the bound.
Values may be sent and summed in bfloat16 or wider, within the bound.
No kernel may reach another device: no remote copies, remote signals or barrier semaphores. Data moves between devices by JAX's collectives and lax.ppermute only.
A program may use at most 64 MiB of HBM per device.

```python
import math
import jax
import jax.numpy as jnp
from jax import lax

BLOCK = 512
ITERS = 6
TOKENS = 16384
D_IN = 16384
D_OUT = 4096


def scale_profile(key, count, rise):
    spread = 0.5 * math.log(10.0)
    base = jax.random.uniform(key, (count,), jnp.float32, -spread, spread)
    ramp = jnp.arange(count, dtype=jnp.float32) / (count - 1)
    return jnp.exp(base + rise * ramp)


def shaped_values(noise, row_key, col_key, rise, factor):
    row_scale = scale_profile(row_key, noise.shape[0], rise)
    col_scale = scale_profile(col_key, noise.shape[1], rise)
    values = factor * noise * row_scale[:, None] * col_scale[None, :]
    return jnp.clip(values, -8.0, 8.0).astype(jnp.bfloat16)


def draw_activations(key, part):
    key = jax.random.fold_in(key, 11)
    row_key, col_key, noise_key = jax.random.split(key, 3)
    noise = jax.random.normal(noise_key, (TOKENS, D_IN), jnp.float32)
    return shaped_values(noise, row_key, col_key, 0.5 * math.log(3.0), 0.2)


def draw_output_grads(key, part):
    key = jax.random.fold_in(key, 23)
    row_key, col_key, noise_key = jax.random.split(key, 3)
    noise = jax.random.normal(noise_key, (TOKENS, D_OUT), jnp.float32)
    return shaped_values(noise, row_key, col_key, 0.5 * math.log(3.0), 0.2)


def level_of(own_key, shape, cuts, smallest, top_value):
    factor_of, own = 1.0, jax.random.fold_in(own_key, 6)
    for dim, parts in cuts:
        draws = jnp.exp(jax.random.uniform(jax.random.fold_in(own, dim), (parts,), jnp.float32, smallest / len(cuts), top_value / len(cuts)))
        factor_of = factor_of * jnp.repeat(draws, shape[dim] // parts).reshape([-1 if axis == dim else 1 for axis in range(len(shape))])
    return factor_of


def centred(rng, dims, scale, reach, cuts=(), kind=jnp.bfloat16):
    drawn = jax.random.normal(rng, dims, jnp.float32) * scale
    if len(cuts) > 0:
        drawn = level_of(rng, dims, cuts, -0.22, 0.18) * drawn
    return jnp.clip(drawn, min=-reach, max=reach).astype(kind)


def setup_inputs(seed: int = 0) -> dict:
    key_list = jax.random.split(jax.random.key(seed), 4)
    return {
        "activations": draw_activations(jax.random.fold_in(key_list[3], 71), 0),
        "output_grads": draw_output_grads(jax.random.fold_in(key_list[3], 71), 0),
        "grad_weight": centred(key_list[2], (D_IN, D_OUT), 16.0, 96.0, ((0, 32), (1, 16))),
    }


DAMP_ROOT = 0.1

def covariance_blocks(data, count):

    def one_block(position):
        columns = lax.dynamic_slice_in_dim(data, position * BLOCK, BLOCK, 1)
        return jnp.dot(columns.T, columns, preferred_element_type=jnp.float32) / TOKENS
    return lax.map(one_block, jnp.arange(count, dtype=jnp.int32))

def invert_block(damped, first_scale):
    identity = jnp.eye(BLOCK, dtype=jnp.float32)
    iterate = identity * first_scale
    damped_half = damped.astype(jnp.bfloat16)
    for sweep in range(ITERS):
        current = iterate.astype(jnp.bfloat16)
        product = jnp.dot(damped_half, current, preferred_element_type=jnp.float32).astype(jnp.bfloat16)
        iterate = 2.0 * iterate - jnp.dot(product, current, preferred_element_type=jnp.float32)
    return iterate.astype(jnp.bfloat16)

def reference(activations, output_grads, grad_weight):
    out_blocks = D_OUT // BLOCK
    covariance_in = covariance_blocks(activations, D_IN // BLOCK)
    covariance_out = covariance_blocks(output_grads, out_blocks)
    traces_in = jnp.trace(covariance_in, axis1=1, axis2=2)
    traces_out = jnp.trace(covariance_out, axis1=1, axis2=2)
    pi_ratio = jnp.sqrt(jnp.sum(traces_in) / D_IN / (jnp.sum(traces_out) / D_OUT))
    damping_in = DAMP_ROOT * pi_ratio
    damping_out = DAMP_ROOT / pi_ratio
    identity = jnp.eye(BLOCK, dtype=jnp.float32)

    def inverse_of(damping):

        def invert_one(entries):
            return invert_block(entries[0] + damping * identity, 1.0 / (entries[1] + BLOCK * damping))
        return invert_one
    inverse_in = lax.map(inverse_of(damping_in), (covariance_in, traces_in))
    inverse_out = lax.map(inverse_of(damping_out), (covariance_out, traces_out))

    def precondition(position):
        weight_rows = lax.dynamic_slice_in_dim(grad_weight, position * BLOCK, BLOCK, 0)
        left_part = jnp.dot(inverse_in[position], weight_rows, preferred_element_type=jnp.float32).astype(jnp.bfloat16)
        pieces = []
        for column_block in range(out_blocks):
            section = left_part[:, column_block * BLOCK:(column_block + 1) * BLOCK]
            pieces.append(jnp.dot(section, inverse_out[column_block], preferred_element_type=jnp.float32))
        return jnp.concatenate(pieces, axis=1).astype(jnp.bfloat16)
    result = lax.map(precondition, jnp.arange(D_IN // BLOCK, dtype=jnp.int32))
    return result.reshape(D_IN, D_OUT)
```

```python
import jax
import jax.numpy as jnp
from jax import lax
from jax.experimental import pallas as pl
from jax.experimental.pallas import tpu as pltpu
from jax.sharding import PartitionSpec as P

ITERS = 6
DAMP_ROOT = 0.1
TILE = 128
CORES = 2
EXTRA = 8
EXTRA_HALF = 16
VMEM_LIMIT = 48 * 1024 * 1024


def tile_plan(count):
    off = [(i, j) for i in range(count) for j in range(i + 1, count)]
    pairs = [(i, i + 1) for i in range(0, count, 2)]
    return off, pairs


def tile_masks():
    rows = lax.broadcasted_iota(jnp.int32, (TILE, TILE), 0)
    cols = lax.broadcasted_iota(jnp.int32, (TILE, TILE), 1)
    return rows, cols


def gram_tiles(left, right, scale):
    return scale * lax.dot_general(
        left, right, (((0,), (0,)), ((), ())), preferred_element_type=jnp.float32
    )


def packed_gram(data_ref, scale, store):
    width = data_ref.shape[1]
    count = width // TILE
    half = width // 2
    low, high = data_ref[:, :half], data_ref[:, half:]
    parts = {
        (0, 0): gram_tiles(low, low, scale),
        (0, 1): gram_tiles(low, high, scale),
        (1, 1): gram_tiles(high, high, scale),
    }
    per = count // 2

    def tile(i, j):
        part = parts[(i // per, j // per)]
        r, c = (i % per) * TILE, (j % per) * TILE
        return part[r : r + TILE, c : c + TILE]

    off, pairs = tile_plan(count)
    rows, cols = tile_masks()
    for position, (i, j) in enumerate(off):
        store(position, tile(i, j))
    for position, (i, j) in enumerate(pairs):
        store(len(off) + position, jnp.where(cols > rows, tile(i, i), tile(j, j)))
    return jnp.concatenate(
        [
            jnp.sum(jnp.where(rows == cols, tile(i, i), 0.0), axis=0, keepdims=True)
            for i in range(count)
        ],
        axis=0,
    )


def unpack_block(packed_ref, diagonal, damping, out_ref):
    count = out_ref.shape[0] // TILE
    off, pairs = tile_plan(count)
    rows, cols = tile_masks()

    def put(i, j, value):
        out_ref[i * TILE : (i + 1) * TILE, j * TILE : (j + 1) * TILE] = value.astype(jnp.bfloat16)

    def fetch(position):
        return packed_ref[position * TILE : (position + 1) * TILE, :].astype(jnp.float32)

    for position, (i, j) in enumerate(off):
        value = fetch(position)
        put(i, j, value)
        put(j, i, value.T)
    for position, (i, j) in enumerate(pairs):
        value = fetch(len(off) + position)
        other = value.T
        damped_i = diagonal[i : i + 1, :] + damping
        damped_j = diagonal[j : j + 1, :] + damping
        put(i, i, jnp.where(rows == cols, damped_i, jnp.where(cols > rows, value, other)))
        put(j, j, jnp.where(rows == cols, damped_j, jnp.where(cols < rows, value, other)))


def total_of(value):
    return jnp.sum(jnp.sum(value, axis=1, keepdims=True), axis=0, keepdims=True)


def gram_in_kernel(tokens, data_ref, grads_ref, out_ref):
    pieces, piece_rows = out_ref.shape[0], out_ref.shape[1] - EXTRA
    per_tile = TILE // piece_rows
    scale = 1.0 / tokens

    def store(position, value):
        for part in range(per_tile):
            out_ref[position * per_tile + part, :piece_rows, :] = value[
                part * piece_rows : (part + 1) * piece_rows
            ]

    diagonal = packed_gram(data_ref, scale, store)
    grads = grads_ref[...].astype(jnp.float32)
    energy = total_of(grads * grads) * scale
    filler = jnp.zeros((EXTRA - diagonal.shape[0] - 1, TILE), jnp.float32)
    extra = jnp.concatenate(
        [diagonal, jnp.broadcast_to(energy, (1, TILE)), filler], axis=0
    )
    for piece in range(pieces):
        out_ref[piece, piece_rows:, :] = extra


def gram_out_kernel(tokens, own_ref, other_ref, keep_ref, send_ref, data_ref, packed_ref):
    half = own_ref.shape[1]
    parity = lax.axis_index("grp") % 2
    core = lax.axis_index("blk") % CORES
    data_ref[:, pl.ds(pl.multiple_of(parity * half, half), half)] = own_ref[...]
    data_ref[:, pl.ds(pl.multiple_of((1 - parity) * half, half), half)] = other_ref[...]

    def store(position, value):
        packed_ref[position * TILE : (position + 1) * TILE, :] = value

    diagonal = packed_gram(data_ref, 1.0 / tokens, store)
    filler = jnp.zeros((EXTRA - diagonal.shape[0], TILE), jnp.float32)
    extra = jnp.concatenate([diagonal, filler], axis=0)
    pieces, piece_rows = keep_ref.shape[0], keep_ref.shape[1] - EXTRA
    share = pieces * piece_rows
    for ref, owner in ((keep_ref, core), (send_ref, 1 - core)):
        for piece in range(pieces):
            start = pl.multiple_of(owner * share + piece * piece_rows, piece_rows)
            ref[piece, :piece_rows, :] = packed_ref[pl.ds(start, piece_rows), :]
            ref[piece, piece_rows:, :] = extra


def add_kernel(left_ref, right_ref, out_ref):
    out_ref[...] = left_ref[...] + right_ref[...]


def sum_pieces(ref):
    total = ref[0]
    for piece in range(1, ref.shape[0]):
        total = total + ref[piece]
    return total


def sum_in_kernel(got_ref, send_ref, extra_ref):
    total = sum_pieces(got_ref)
    rows = send_ref.shape[1]
    rounded = total[:rows].astype(jnp.bfloat16)
    for piece in range(send_ref.shape[0]):
        send_ref[piece] = rounded
    extra_ref[...] = total[rows:]


def split_rows(value):
    high = value.astype(jnp.bfloat16).astype(jnp.float32)
    rest = value - high
    middle = rest.astype(jnp.bfloat16).astype(jnp.float32)
    return [high, middle, rest - middle]


def sum_out_kernel(count, got_ref, extra_in_ref, send_ref, extra_ref):
    total = sum_pieces(got_ref)
    rows = send_ref.shape[1] - EXTRA_HALF
    trace_in = jnp.broadcast_to(total_of(extra_in_ref[:count, :]), (1, TILE))
    energy_out = extra_in_ref[count : count + 1, :]
    scalars = split_rows(trace_in) + split_rows(energy_out)
    filler = jnp.zeros((EXTRA_HALF - len(scalars), TILE), jnp.float32)
    block = jnp.concatenate([total[:rows]] + scalars + [filler], axis=0).astype(jnp.bfloat16)
    for piece in range(send_ref.shape[0]):
        send_ref[piece] = block
    extra_ref[...] = total[rows:]


def invert_kernel(
    got_in_ref,
    got_out_ref,
    core_out_ref,
    extra_in_ref,
    extra_out_ref,
    weight_ref,
    other_weight_ref,
    result_ref,
    packed_ref,
    damped_in_ref,
    damped_out_ref,
    iterate_in_ref,
    iterate_out_ref,
    weight_block_ref,
):
    width = damped_in_ref.shape[0]
    count = width // TILE
    half = weight_ref.shape[1]
    parity = lax.axis_index("grp") % 2
    core = lax.axis_index("blk") % CORES
    pieces = got_out_ref.shape[0]
    piece_rows = got_out_ref.shape[1] - EXTRA_HALF
    own_column = pl.ds(pl.multiple_of(parity * half, half), half)
    other_column = pl.ds(pl.multiple_of((1 - parity) * half, half), half)
    weight_block_ref[:, own_column] = weight_ref[...]
    weight_block_ref[:, other_column] = other_weight_ref[...]

    scalars = jnp.zeros((EXTRA_HALF, TILE), jnp.float32)
    for ref in (got_out_ref, core_out_ref):
        for piece in range(pieces):
            scalars = scalars + ref[piece, piece_rows:, :].astype(jnp.float32)
    sum_in = scalars[0:1] + scalars[1:2] + scalars[2:3]
    sum_out = scalars[3:4] + scalars[4:5] + scalars[5:6]
    owners = pieces * CORES
    blocks_out = lax.axis_size("grp") // 2
    pi_ratio = jnp.sqrt((sum_in / (owners * width)) / (sum_out / (blocks_out * width)))
    damping_in = DAMP_ROOT * pi_ratio
    damping_out = DAMP_ROOT / pi_ratio
    diagonal_in = extra_in_ref[:count, :]
    diagonal_out = extra_out_ref[:count, :]
    scale_in = 1.0 / (total_of(diagonal_in) + width * damping_in)
    scale_out = 1.0 / (total_of(diagonal_out) + width * damping_out)

    in_rows = got_in_ref.shape[1]
    for piece in range(got_in_ref.shape[0]):
        packed_ref[piece * in_rows : (piece + 1) * in_rows, :] = got_in_ref[piece]
    unpack_block(packed_ref, diagonal_in, damping_in, damped_in_ref)
    share = pieces * piece_rows
    for ref, owner in ((got_out_ref, core), (core_out_ref, 1 - core)):
        for piece in range(pieces):
            start = pl.multiple_of(owner * share + piece * piece_rows, piece_rows)
            packed_ref[pl.ds(start, piece_rows), :] = ref[piece, :piece_rows, :]
    unpack_block(packed_ref, diagonal_out, damping_out, damped_out_ref)

    chains = (
        (damped_in_ref, iterate_in_ref, scale_in),
        (damped_out_ref, iterate_out_ref, scale_out),
    )
    rows, cols = tile_masks()
    for damped, iterate, scale in chains:
        factor = scale.astype(jnp.bfloat16).astype(jnp.float32)
        twice = jnp.where(rows == cols, 2.0 * scale, 0.0)
        for i in range(count):
            for j in range(count):
                place = (slice(i * TILE, (i + 1) * TILE), slice(j * TILE, (j + 1) * TILE))
                product = (damped[place].astype(jnp.float32) * factor).astype(jnp.bfloat16)
                moved = product.astype(jnp.float32) * factor
                iterate[place] = (twice - moved) if i == j else -moved

    def sweep(step, carry):
        currents = [iterate[...].astype(jnp.bfloat16) for _, iterate, _ in chains]
        products = [
            jnp.dot(damped[...], current, preferred_element_type=jnp.float32).astype(jnp.bfloat16)
            for (damped, _, _), current in zip(chains, currents)
        ]
        for (_, iterate, _), product, current in zip(chains, products, currents):
            iterate[...] = 2.0 * iterate[...] - jnp.dot(
                product, current, preferred_element_type=jnp.float32
            )
        return carry

    lax.fori_loop(0, ITERS - 1, sweep, 0)
    inverse_in = iterate_in_ref[...].astype(jnp.bfloat16)
    left = jnp.dot(inverse_in, weight_block_ref[...], preferred_element_type=jnp.float32)
    right = iterate_out_ref[:, own_column].astype(jnp.bfloat16)
    result_ref[...] = jnp.dot(
        left.astype(jnp.bfloat16), right, preferred_element_type=jnp.float32
    ).astype(jnp.bfloat16)


VMEM_SPEC = pl.BlockSpec(memory_space=pltpu.VMEM)


def local_call(kernel, name, operands, outs, scratch=(), flops=0):
    multiple = isinstance(outs, tuple)
    listed = outs if multiple else (outs,)
    moved = sum(a.size * a.dtype.itemsize for a in operands + tuple(listed))
    return pl.pallas_call(
        kernel,
        out_shape=outs,
        in_specs=[VMEM_SPEC] * len(operands),
        out_specs=tuple([VMEM_SPEC] * len(listed)) if multiple else VMEM_SPEC,
        scratch_shapes=list(scratch),
        compiler_params=pltpu.CompilerParams(vmem_limit_bytes=VMEM_LIMIT),
        cost_estimate=pl.CostEstimate(flops=flops, bytes_accessed=moved, transcendentals=0),
        name=name,
    )(*operands)


def shape_of(*dims, dtype=jnp.float32):
    return jax.ShapeDtypeStruct(dims, dtype)


def exchange(value, axis, groups=None):
    return lax.all_to_all(value, axis, 0, 0, tiled=True, axis_index_groups=groups)


def shards(activations, output_grads, grad_weight):
    groups = lax.axis_size("grp")
    owners = lax.axis_size("blk")
    width = grad_weight.shape[0]
    half = grad_weight.shape[1]
    count = width // TILE
    packed_rows = width * width // (2 * TILE)
    total_tokens = activations.shape[0] * groups
    in_rows = packed_rows // groups
    out_pieces = owners // CORES
    out_rows = packed_rows // owners
    partner = [(source, source ^ 1) for source in range(groups)]
    sibling = [(source, source ^ 1) for source in range(owners)]
    same_core = [[piece * CORES + core for piece in range(out_pieces)] for core in range(CORES)]

    other_grads = lax.ppermute(output_grads, "grp", partner)
    send_in = local_call(
        lambda *refs: gram_in_kernel(total_tokens, *refs),
        "gram_in",
        (activations, output_grads),
        shape_of(groups, in_rows + EXTRA, TILE),
        flops=2 * activations.shape[0] * width * width,
    )
    got_in = exchange(send_in, "grp")

    keep, give = local_call(
        lambda *refs: gram_out_kernel(total_tokens, *refs),
        "gram_out",
        (output_grads, other_grads),
        (shape_of(out_pieces, out_rows + EXTRA, TILE),) * 2,
        scratch=[
            pltpu.VMEM((output_grads.shape[0], width), jnp.bfloat16),
            pltpu.VMEM((packed_rows, TILE), jnp.float32),
        ],
        flops=2 * output_grads.shape[0] * width * width,
    )
    taken = lax.ppermute(give, "blk", sibling)
    send_out = local_call(add_kernel, "add_cores", (keep, taken), shape_of(*keep.shape))
    got_out = exchange(send_out, "blk", same_core)

    all_in, extra_in = local_call(
        sum_in_kernel,
        "sum_in",
        (got_in,),
        (shape_of(groups, in_rows, TILE, dtype=jnp.bfloat16), shape_of(EXTRA, TILE)),
    )
    all_in = exchange(all_in, "grp")
    all_out, extra_out = local_call(
        lambda *refs: sum_out_kernel(count, *refs),
        "sum_out",
        (got_out, extra_in),
        (
            shape_of(out_pieces, out_rows + EXTRA_HALF, TILE, dtype=jnp.bfloat16),
            shape_of(EXTRA, TILE),
        ),
    )
    all_out = exchange(all_out, "blk", same_core)
    core_out = lax.ppermute(all_out, "blk", sibling)
    other_weight = lax.ppermute(grad_weight, "grp", partner)

    block = (width, width)
    return local_call(
        invert_kernel,
        "invert",
        (all_in, all_out, core_out, extra_in, extra_out, grad_weight, other_weight),
        shape_of(width, half, dtype=jnp.bfloat16),
        scratch=[
            pltpu.VMEM((packed_rows, TILE), jnp.bfloat16),
            pltpu.VMEM(block, jnp.bfloat16),
            pltpu.VMEM(block, jnp.bfloat16),
            pltpu.VMEM(block, jnp.float32),
            pltpu.VMEM(block, jnp.float32),
            pltpu.VMEM(block, jnp.bfloat16),
        ],
        flops=2 * (4 * (ITERS - 1) + 2) * width * width * width,
    )


def solution(mesh):
    in_specs = (P("grp", "blk"), P("blk", "grp"), P("blk", "grp"))
    out_specs = P("blk", "grp")
    return jax.shard_map(shards, mesh=mesh, in_specs=in_specs, out_specs=out_specs, check_vma=False)
```

```python
import jax
import jax.numpy as jnp
from jax import lax
from jax.experimental import pallas as pl
from jax.experimental.pallas import tpu as pltpu
from jax.sharding import PartitionSpec as P

ITERS = 6
DAMP_ROOT = 0.1
TILE = 128
CORES = 2
RING = 4
EXTRA = 8
EXTRA_HALF = 16
VMEM_LIMIT = 48 * 1024 * 1024


def tile_plan(count):
    off = [(i, j) for i in range(count) for j in range(i + 1, count)]
    pairs = [(i, i + 1) for i in range(0, count, 2)]
    return off, pairs


def tile_masks():
    rows = lax.broadcasted_iota(jnp.int32, (TILE, TILE), 0)
    cols = lax.broadcasted_iota(jnp.int32, (TILE, TILE), 1)
    return rows, cols


def gram_tiles(left, right, scale):
    return scale * lax.dot_general(
        left, right, (((0,), (0,)), ((), ())), preferred_element_type=jnp.float32
    )


def packed_gram(data_ref, scale, store):
    width = data_ref.shape[1]
    count = width // TILE
    half = width // 2
    low, high = data_ref[:, :half], data_ref[:, half:]
    parts = {
        (0, 0): gram_tiles(low, low, scale),
        (0, 1): gram_tiles(low, high, scale),
        (1, 1): gram_tiles(high, high, scale),
    }
    per = count // 2

    def tile(i, j):
        part = parts[(i // per, j // per)]
        r, c = (i % per) * TILE, (j % per) * TILE
        return part[r : r + TILE, c : c + TILE]

    off, pairs = tile_plan(count)
    rows, cols = tile_masks()
    for position, (i, j) in enumerate(off):
        store(position, tile(i, j))
    for position, (i, j) in enumerate(pairs):
        store(len(off) + position, jnp.where(cols > rows, tile(i, i), tile(j, j)))
    return jnp.concatenate(
        [
            jnp.sum(jnp.where(rows == cols, tile(i, i), 0.0), axis=0, keepdims=True)
            for i in range(count)
        ],
        axis=0,
    )


def unpack_block(fetch, out_ref):
    count = out_ref.shape[0] // TILE
    off, pairs = tile_plan(count)
    rows, cols = tile_masks()

    def put(i, j, value):
        out_ref[i * TILE : (i + 1) * TILE, j * TILE : (j + 1) * TILE] = value.astype(jnp.bfloat16)

    for position, (i, j) in enumerate(off):
        value = fetch(position).astype(jnp.float32)
        put(i, j, value)
        put(j, i, value.T)
    for position, (i, j) in enumerate(pairs):
        value = fetch(len(off) + position).astype(jnp.float32)
        other = value.T
        put(i, i, jnp.where(cols > rows, value, other))
        put(j, j, jnp.where(cols < rows, value, other))


def put_diagonal(diagonal, damping, out_ref):
    rows, cols = tile_masks()
    for i in range(out_ref.shape[0] // TILE):
        place = (slice(i * TILE, (i + 1) * TILE),) * 2
        damped = diagonal[i : i + 1, :] + damping
        tile = out_ref[place].astype(jnp.float32)
        out_ref[place] = jnp.where(rows == cols, damped, tile).astype(jnp.bfloat16)


def total_of(value):
    return jnp.sum(jnp.sum(value, axis=1, keepdims=True), axis=0, keepdims=True)


def gram_in_kernel(tokens, data_ref, grads_ref, out_ref):
    pieces, piece_rows = out_ref.shape[0], out_ref.shape[1] - EXTRA
    per_tile = TILE // piece_rows
    scale = 1.0 / tokens

    def store(position, value):
        for part in range(per_tile):
            out_ref[position * per_tile + part, :piece_rows, :] = value[
                part * piece_rows : (part + 1) * piece_rows
            ]

    diagonal = packed_gram(data_ref, scale, store)
    grads = grads_ref[...].astype(jnp.float32)
    energy = total_of(grads * grads) * scale
    filler = jnp.zeros((EXTRA - diagonal.shape[0] - 1, TILE), jnp.float32)
    extra = jnp.concatenate(
        [diagonal, jnp.broadcast_to(energy, (1, TILE)), filler], axis=0
    )
    for piece in range(pieces):
        out_ref[piece, piece_rows:, :] = extra


def gram_out_kernel(tokens, own_ref, other_ref, keep_ref, send_ref, data_ref, packed_ref):
    half = own_ref.shape[1]
    parity = lax.axis_index("grp") % 2
    core = lax.axis_index("blk") % CORES
    data_ref[:, pl.ds(pl.multiple_of(parity * half, half), half)] = own_ref[...]
    data_ref[:, pl.ds(pl.multiple_of((1 - parity) * half, half), half)] = other_ref[...]

    def store(position, value):
        packed_ref[position * TILE : (position + 1) * TILE, :] = value

    diagonal = packed_gram(data_ref, 1.0 / tokens, store)
    filler = jnp.zeros((EXTRA - diagonal.shape[0], TILE), jnp.float32)
    extra = jnp.concatenate([diagonal, filler], axis=0)
    share = keep_ref.shape[0] - EXTRA
    for ref, owner in ((keep_ref, core), (send_ref, 1 - core)):
        start = pl.multiple_of(owner * share, share)
        ref[:share, :] = packed_ref[pl.ds(start, share), :]
        ref[share:, :] = extra


def along_x():
    return lax.axis_index("blk") // (RING * CORES)


def add_cores_kernel(left_ref, right_ref, *out_refs):
    rows = out_refs[0].shape[0] - EXTRA
    share = left_ref.shape[0] - EXTRA
    extra = left_ref[share:, :] + right_ref[share:, :]
    for step, ref in enumerate(out_refs):
        place = pl.ds(pl.multiple_of((along_x() ^ step) * rows, rows), rows)
        ref[:rows, :] = left_ref[place, :] + right_ref[place, :]
        ref[rows:, :] = extra


def sum_ring(refs):
    return (refs[0][...] + refs[1][...]) + (refs[2][...] + refs[3][...])


def sum_pieces(ref):
    total = ref[0]
    for piece in range(1, ref.shape[0]):
        total = total + ref[piece]
    return total


def split_rows(value):
    high = value.astype(jnp.bfloat16).astype(jnp.float32)
    rest = value - high
    middle = rest.astype(jnp.bfloat16).astype(jnp.float32)
    return [high, middle, rest - middle]


def sum_both_kernel(count, got_ref, *refs):
    *got_refs, send_ref, extra_in_ref, out_ref = refs
    total = sum_pieces(got_ref)
    rows = send_ref.shape[1]
    rounded = total[:rows].astype(jnp.bfloat16)
    for piece in range(send_ref.shape[0]):
        send_ref[piece] = rounded
    extra = total[rows:]
    extra_in_ref[...] = extra
    total = sum_ring(got_refs)
    rows = total.shape[0] - EXTRA
    trace_in = jnp.broadcast_to(total_of(extra[:count]), (1, TILE))
    energy_out = extra[count : count + 1]
    filler = jnp.zeros((EXTRA - count - 2, TILE), jnp.float32)
    out_ref[...] = jnp.concatenate(
        [total[: rows + count], trace_in, energy_out, filler], axis=0
    )


def sum_y_kernel(count, *refs):
    *got_refs, piece_ref, extra_ref = refs
    total = sum_ring(got_refs)
    rows = total.shape[0] - EXTRA
    extra = total[rows:]
    scalars = split_rows(extra[count : count + 1]) + split_rows(extra[count + 1 : count + 2])
    filler = jnp.zeros((EXTRA_HALF - len(scalars), TILE), jnp.float32)
    piece_ref[...] = jnp.concatenate([total[:rows]] + scalars + [filler], axis=0).astype(
        jnp.bfloat16
    )
    extra_ref[...] = extra


def join_kernel(*refs):
    *got_refs, out_ref = refs
    for step, ref in enumerate(got_refs):
        out_ref[along_x() ^ step] = ref[...]


def unpack_in_kernel(got_ref, out_ref):
    rows = got_ref.shape[1]
    per_tile = TILE // rows
    unpack_block(
        lambda position: jnp.concatenate(
            [got_ref[position * per_tile + part] for part in range(per_tile)], axis=0
        ),
        out_ref,
    )


def invert_kernel(
    damped_in_ref,
    got_out_ref,
    core_out_ref,
    extra_in_ref,
    extra_out_ref,
    weight_ref,
    other_weight_ref,
    result_ref,
    packed_ref,
    full_in_ref,
    damped_out_ref,
    iterate_in_ref,
    iterate_out_ref,
    weight_block_ref,
):
    width = damped_in_ref.shape[0]
    count = width // TILE
    half = weight_ref.shape[1]
    parity = lax.axis_index("grp") % 2
    core = lax.axis_index("blk") % CORES
    pieces, rows_out = got_out_ref.shape[0], got_out_ref.shape[1] - EXTRA_HALF
    own_column = pl.ds(pl.multiple_of(parity * half, half), half)
    other_column = pl.ds(pl.multiple_of((1 - parity) * half, half), half)
    weight_block_ref[:, own_column] = weight_ref[...]
    weight_block_ref[:, other_column] = other_weight_ref[...]

    scalars = jnp.zeros((EXTRA_HALF, TILE), jnp.float32)
    for piece in range(pieces):
        for ref in (got_out_ref, core_out_ref):
            scalars = scalars + ref[piece, rows_out:, :].astype(jnp.float32)
    sum_in = scalars[0:1] + scalars[1:2] + scalars[2:3]
    sum_out = scalars[3:4] + scalars[4:5] + scalars[5:6]
    owners = lax.axis_size("blk")
    blocks_out = lax.axis_size("grp") // 2
    pi_ratio = jnp.sqrt((sum_in / (owners * width)) / (sum_out / (blocks_out * width)))
    damping_in = DAMP_ROOT * pi_ratio
    damping_out = DAMP_ROOT / pi_ratio
    diagonal_in = extra_in_ref[:count, :]
    diagonal_out = extra_out_ref[:count, :]
    scale_in = 1.0 / (total_of(diagonal_in) + width * damping_in)
    scale_out = 1.0 / (total_of(diagonal_out) + width * damping_out)

    full_in_ref[...] = damped_in_ref[...]
    put_diagonal(diagonal_in, damping_in, full_in_ref)
    for ref, owner in ((got_out_ref, core), (core_out_ref, 1 - core)):
        for piece in range(pieces):
            packed_ref[owner * pieces + piece] = ref[piece, :rows_out, :]
    unpack_block(lambda position: packed_ref[position], damped_out_ref)
    put_diagonal(diagonal_out, damping_out, damped_out_ref)

    chains = (
        (full_in_ref, iterate_in_ref, scale_in),
        (damped_out_ref, iterate_out_ref, scale_out),
    )
    rows, cols = tile_masks()
    for damped, iterate, scale in chains:
        factor = scale.astype(jnp.bfloat16).astype(jnp.float32)
        twice = jnp.where(rows == cols, 2.0 * scale, 0.0)
        for i in range(count):
            for j in range(count):
                place = (slice(i * TILE, (i + 1) * TILE), slice(j * TILE, (j + 1) * TILE))
                product = (damped[place].astype(jnp.float32) * factor).astype(jnp.bfloat16)
                moved = product.astype(jnp.float32) * factor
                iterate[place] = (twice - moved) if i == j else -moved

    def sweep(step, carry):
        currents = [iterate[...].astype(jnp.bfloat16) for _, iterate, _ in chains]
        products = [
            jnp.dot(damped[...], current, preferred_element_type=jnp.float32).astype(jnp.bfloat16)
            for (damped, _, _), current in zip(chains, currents)
        ]
        for (_, iterate, _), product, current in zip(chains, products, currents):
            iterate[...] = 2.0 * iterate[...] - jnp.dot(
                product, current, preferred_element_type=jnp.float32
            )
        return carry

    lax.fori_loop(0, ITERS - 1, sweep, 0)
    inverse_in = iterate_in_ref[...].astype(jnp.bfloat16)
    left = jnp.dot(inverse_in, weight_block_ref[...], preferred_element_type=jnp.float32)
    right = iterate_out_ref[:, own_column].astype(jnp.bfloat16)
    result_ref[...] = jnp.dot(
        left.astype(jnp.bfloat16), right, preferred_element_type=jnp.float32
    ).astype(jnp.bfloat16)


VMEM_SPEC = pl.BlockSpec(memory_space=pltpu.VMEM)


def local_call(kernel, name, operands, outs, scratch=(), flops=0):
    multiple = isinstance(outs, tuple)
    listed = outs if multiple else (outs,)
    moved = sum(a.size * a.dtype.itemsize for a in operands + tuple(listed))
    return pl.pallas_call(
        kernel,
        out_shape=outs,
        in_specs=[VMEM_SPEC] * len(operands),
        out_specs=tuple([VMEM_SPEC] * len(listed)) if multiple else VMEM_SPEC,
        scratch_shapes=list(scratch),
        compiler_params=pltpu.CompilerParams(vmem_limit_bytes=VMEM_LIMIT),
        cost_estimate=pl.CostEstimate(flops=flops, bytes_accessed=moved, transcendentals=0),
        name=name,
    )(*operands)


def shape_of(*dims, dtype=jnp.float32):
    return jax.ShapeDtypeStruct(dims, dtype)


def exchange(value, axis, groups=None):
    return lax.all_to_all(value, axis, 0, 0, tiled=True, axis_index_groups=groups)


def swap_core(value):
    pairs = [(place, place ^ 1) for place in range(lax.axis_size("blk"))]
    return lax.ppermute(value, "blk", pairs)


def swap_along(value, stride, step):
    pairs = [(place, place ^ (stride * step)) for place in range(lax.axis_size("blk"))]
    return lax.ppermute(value, "blk", pairs)


def swap_half(value):
    pairs = [(place, place ^ 1) for place in range(lax.axis_size("grp"))]
    return lax.ppermute(value, "grp", pairs)


def shards(activations, output_grads, grad_weight):
    groups = lax.axis_size("grp")
    width = grad_weight.shape[0]
    half = grad_weight.shape[1]
    count = width // TILE
    packed_rows = width * width // (2 * TILE)
    total_tokens = activations.shape[0] * groups
    in_rows = packed_rows // groups
    share_rows = packed_rows // CORES
    piece_rows = share_rows // RING
    y_stride, x_stride = CORES, CORES * RING
    half_type = jnp.bfloat16

    other_grads = swap_half(output_grads)
    send_in = local_call(
        lambda *refs: gram_in_kernel(total_tokens, *refs),
        "gram_in",
        (activations, output_grads),
        shape_of(groups, in_rows + EXTRA, TILE),
        flops=2 * activations.shape[0] * width * width,
    )
    got_in = exchange(send_in, "grp")

    keep, give = local_call(
        lambda *refs: gram_out_kernel(total_tokens, *refs),
        "gram_out",
        (output_grads, other_grads),
        (shape_of(share_rows + EXTRA, TILE),) * 2,
        scratch=[
            pltpu.VMEM((output_grads.shape[0], width), half_type),
            pltpu.VMEM((packed_rows, TILE), jnp.float32),
        ],
        flops=200 * output_grads.shape[0] * width * width,
    )
    keep, *gives = local_call(
        add_cores_kernel,
        "add_cores",
        (keep, swap_core(give)),
        (shape_of(piece_rows + EXTRA, TILE),) * RING,
    )
    taken = [swap_along(give, x_stride, step + 1) for step, give in enumerate(gives)]
    to_all_in, extra_in, part_y = local_call(
        lambda *refs: sum_both_kernel(count, *refs),
        "sum_both",
        (got_in, keep, *taken),
        (
            shape_of(groups, in_rows, TILE, dtype=half_type),
            shape_of(EXTRA, TILE),
            shape_of(piece_rows + EXTRA, TILE),
        ),
    )
    all_in = exchange(to_all_in, "grp")
    taken = [swap_along(part_y, y_stride, step) for step in range(1, RING)]
    piece, extra_out = local_call(
        lambda *refs: sum_y_kernel(count, *refs),
        "sum_y",
        (part_y, *taken),
        (shape_of(piece_rows + EXTRA_HALF, TILE, dtype=half_type), shape_of(EXTRA, TILE)),
    )
    taken = [swap_along(piece, x_stride, step) for step in range(1, RING)]
    all_out = local_call(
        join_kernel,
        "join_x",
        (piece, *taken),
        shape_of(RING, piece_rows + EXTRA_HALF, TILE, dtype=half_type),
    )
    core_out = swap_core(all_out)
    other_weight = swap_half(grad_weight)

    block = (width, width)
    damped_in = local_call(unpack_in_kernel, "unpack_in", (all_in,), shape_of(*block, dtype=half_type))
    return local_call(
        invert_kernel,
        "invert",
        (damped_in, all_out, core_out, extra_in, extra_out, grad_weight, other_weight),
        shape_of(width, half, dtype=half_type),
        scratch=[
            pltpu.VMEM((CORES * RING, piece_rows, TILE), half_type),
            pltpu.VMEM(block, half_type),
            pltpu.VMEM(block, half_type),
            pltpu.VMEM(block, jnp.float32),
            pltpu.VMEM(block, jnp.float32),
            pltpu.VMEM(block, half_type),
        ],
        flops=2 * (4 * (ITERS - 1) + 2) * width * width * width,
    )


def solution(mesh):
    in_specs = (P("grp", "blk"), P("blk", "grp"), P("blk", "grp"))
    out_specs = P("blk", "grp")
    return jax.shard_map(shards, mesh=mesh, in_specs=in_specs, out_specs=out_specs, check_vma=False)
```

```python
import jax
import jax.numpy as jnp
from jax import lax
from jax.experimental import pallas as pl
from jax.experimental.pallas import tpu as pltpu
from jax.sharding import PartitionSpec as P

ITERS = 6
DAMP_ROOT = 0.1
TILE = 128
CORES = 2
RING = 4
EXTRA = 8
EXTRA_HALF = 16
LATE_START = 10**10
VMEM_LIMIT = 48 * 1024 * 1024


def tile_plan(count):
    off = [(i, j) for i in range(count) for j in range(i + 1, count)]
    pairs = [(i, i + 1) for i in range(0, count, 2)]
    return off, pairs


def tile_masks():
    rows = lax.broadcasted_iota(jnp.int32, (TILE, TILE), 0)
    cols = lax.broadcasted_iota(jnp.int32, (TILE, TILE), 1)
    return rows, cols


def gram_tiles(left, right, scale):
    return scale * lax.dot_general(
        left, right, (((0,), (0,)), ((), ())), preferred_element_type=jnp.float32
    )


def packed_gram(data_ref, scale, store):
    width = data_ref.shape[1]
    count = width // TILE
    half = width // 2
    low, high = data_ref[:, :half], data_ref[:, half:]
    parts = {
        (0, 0): gram_tiles(low, low, scale),
        (0, 1): gram_tiles(low, high, scale),
        (1, 1): gram_tiles(high, high, scale),
    }
    per = count // 2

    def tile(i, j):
        part = parts[(i // per, j // per)]
        r, c = (i % per) * TILE, (j % per) * TILE
        return part[r : r + TILE, c : c + TILE]

    off, pairs = tile_plan(count)
    rows, cols = tile_masks()
    for position, (i, j) in enumerate(off):
        store(position, tile(i, j))
    for position, (i, j) in enumerate(pairs):
        store(len(off) + position, jnp.where(cols > rows, tile(i, i), tile(j, j)))
    return jnp.concatenate(
        [
            jnp.sum(jnp.where(rows == cols, tile(i, i), 0.0), axis=0, keepdims=True)
            for i in range(count)
        ],
        axis=0,
    )


def unpack_block(fetch, out_ref):
    count = out_ref.shape[0] // TILE
    off, pairs = tile_plan(count)
    rows, cols = tile_masks()

    def put(i, j, value):
        out_ref[i * TILE : (i + 1) * TILE, j * TILE : (j + 1) * TILE] = value.astype(jnp.bfloat16)

    for position, (i, j) in enumerate(off):
        value = fetch(position).astype(jnp.float32)
        put(i, j, value)
        put(j, i, value.T)
    for position, (i, j) in enumerate(pairs):
        value = fetch(len(off) + position).astype(jnp.float32)
        other = value.T
        put(i, i, jnp.where(cols > rows, value, other))
        put(j, j, jnp.where(cols < rows, value, other))


def put_diagonal(diagonal, damping, out_ref):
    rows, cols = tile_masks()
    for i in range(out_ref.shape[0] // TILE):
        place = (slice(i * TILE, (i + 1) * TILE),) * 2
        damped = diagonal[i : i + 1, :] + damping
        tile = out_ref[place].astype(jnp.float32)
        out_ref[place] = jnp.where(rows == cols, damped, tile).astype(jnp.bfloat16)


def total_of(value):
    return jnp.sum(jnp.sum(value, axis=1, keepdims=True), axis=0, keepdims=True)


def gram_in_kernel(tokens, data_ref, grads_ref, out_ref):
    pieces, piece_rows = out_ref.shape[0], out_ref.shape[1] - EXTRA
    per_tile = TILE // piece_rows
    scale = 1.0 / tokens

    def store(position, value):
        for part in range(per_tile):
            out_ref[position * per_tile + part, :piece_rows, :] = value[
                part * piece_rows : (part + 1) * piece_rows
            ]

    diagonal = packed_gram(data_ref, scale, store)
    grads = grads_ref[...].astype(jnp.float32)
    energy = total_of(grads * grads) * scale
    filler = jnp.zeros((EXTRA - diagonal.shape[0] - 1, TILE), jnp.float32)
    extra = jnp.concatenate(
        [diagonal, jnp.broadcast_to(energy, (1, TILE)), filler], axis=0
    )
    for piece in range(pieces):
        out_ref[piece, piece_rows:, :] = extra


def gram_out_kernel(tokens, own_ref, other_ref, keep_ref, send_ref, data_ref, packed_ref):
    half = own_ref.shape[1]
    parity = lax.axis_index("grp") % 2
    core = lax.axis_index("blk") % CORES
    data_ref[:, pl.ds(pl.multiple_of(parity * half, half), half)] = own_ref[...]
    data_ref[:, pl.ds(pl.multiple_of((1 - parity) * half, half), half)] = other_ref[...]

    def store(position, value):
        packed_ref[position * TILE : (position + 1) * TILE, :] = value

    diagonal = packed_gram(data_ref, 1.0 / tokens, store)
    filler = jnp.zeros((EXTRA - diagonal.shape[0], TILE), jnp.float32)
    extra = jnp.concatenate([diagonal, filler], axis=0)
    share = keep_ref.shape[0] - EXTRA
    for ref, owner in ((keep_ref, core), (send_ref, 1 - core)):
        start = pl.multiple_of(owner * share, share)
        ref[:share, :] = packed_ref[pl.ds(start, share), :]
        ref[share:, :] = extra


def along_x():
    return lax.axis_index("blk") // (RING * CORES)


def add_cores_kernel(left_ref, right_ref, *out_refs):
    rows = out_refs[0].shape[0] - EXTRA
    share = left_ref.shape[0] - EXTRA
    extra = left_ref[share:, :] + right_ref[share:, :]
    for step, ref in enumerate(out_refs):
        place = pl.ds(pl.multiple_of((along_x() ^ step) * rows, rows), rows)
        ref[:rows, :] = left_ref[place, :] + right_ref[place, :]
        ref[rows:, :] = extra


def sum_ring(refs):
    return (refs[0][...] + refs[1][...]) + (refs[2][...] + refs[3][...])


def sum_pieces(ref):
    total = ref[0]
    for piece in range(1, ref.shape[0]):
        total = total + ref[piece]
    return total


def split_rows(value):
    high = value.astype(jnp.bfloat16).astype(jnp.float32)
    rest = value - high
    middle = rest.astype(jnp.bfloat16).astype(jnp.float32)
    return [high, middle, rest - middle]


def sum_both_kernel(count, got_ref, *refs):
    *got_refs, send_ref, extra_in_ref, out_ref = refs
    total = sum_pieces(got_ref)
    rows = send_ref.shape[1]
    rounded = total[:rows].astype(jnp.bfloat16)
    for piece in range(send_ref.shape[0]):
        send_ref[piece] = rounded
    extra = total[rows:]
    extra_in_ref[...] = extra
    total = sum_ring(got_refs)
    rows = total.shape[0] - EXTRA
    trace_in = jnp.broadcast_to(total_of(extra[:count]), (1, TILE))
    energy_out = extra[count : count + 1]
    filler = jnp.zeros((EXTRA - count - 2, TILE), jnp.float32)
    out_ref[...] = jnp.concatenate(
        [total[: rows + count], trace_in, energy_out, filler], axis=0
    )


def sum_y_kernel(count, *refs):
    *got_refs, send_ref, extra_ref = refs
    total = sum_ring(got_refs)
    rows = total.shape[0] - EXTRA
    extra = total[rows:]
    scalars = split_rows(extra[count : count + 1]) + split_rows(extra[count + 1 : count + 2])
    filler = jnp.zeros((EXTRA_HALF - len(scalars), TILE), jnp.float32)
    block = jnp.concatenate([total[:rows]] + scalars + [filler], axis=0).astype(jnp.bfloat16)
    for piece in range(send_ref.shape[0]):
        send_ref[piece] = block
    extra_ref[...] = extra


def unpack_in_kernel(got_ref, out_ref):
    rows = got_ref.shape[1]
    per_tile = TILE // rows
    unpack_block(
        lambda position: jnp.concatenate(
            [got_ref[position * per_tile + part] for part in range(per_tile)], axis=0
        ),
        out_ref,
    )


def invert_kernel(
    damped_in_ref,
    got_out_ref,
    extra_in_ref,
    extra_out_ref,
    weight_ref,
    other_weight_ref,
    result_ref,
    full_in_ref,
    damped_out_ref,
    iterate_in_ref,
    iterate_out_ref,
    weight_block_ref,
):
    width = damped_in_ref.shape[0]
    count = width // TILE
    half = weight_ref.shape[1]
    parity = lax.axis_index("grp") % 2
    pieces, rows_out = got_out_ref.shape[0], got_out_ref.shape[1] - EXTRA_HALF
    own_column = pl.ds(pl.multiple_of(parity * half, half), half)
    other_column = pl.ds(pl.multiple_of((1 - parity) * half, half), half)
    weight_block_ref[:, own_column] = weight_ref[...]
    weight_block_ref[:, other_column] = other_weight_ref[...]

    scalars = jnp.zeros((EXTRA_HALF, TILE), jnp.float32)
    for piece in range(pieces):
        scalars = scalars + got_out_ref[piece, rows_out:, :].astype(jnp.float32)
    sum_in = scalars[0:1] + scalars[1:2] + scalars[2:3]
    sum_out = scalars[3:4] + scalars[4:5] + scalars[5:6]
    owners = lax.axis_size("blk")
    blocks_out = lax.axis_size("grp") // 2
    pi_ratio = jnp.sqrt((sum_in / (owners * width)) / (sum_out / (blocks_out * width)))
    damping_in = DAMP_ROOT * pi_ratio
    damping_out = DAMP_ROOT / pi_ratio
    diagonal_in = extra_in_ref[:count, :]
    diagonal_out = extra_out_ref[:count, :]
    scale_in = 1.0 / (total_of(diagonal_in) + width * damping_in)
    scale_out = 1.0 / (total_of(diagonal_out) + width * damping_out)

    full_in_ref[...] = damped_in_ref[...]
    put_diagonal(diagonal_in, damping_in, full_in_ref)
    unpack_block(
        lambda position: got_out_ref[
            position % RING * CORES + position // RING, :rows_out, :
        ],
        damped_out_ref,
    )
    put_diagonal(diagonal_out, damping_out, damped_out_ref)

    chains = (
        (full_in_ref, iterate_in_ref, scale_in),
        (damped_out_ref, iterate_out_ref, scale_out),
    )
    rows, cols = tile_masks()
    for damped, iterate, scale in chains:
        factor = scale.astype(jnp.bfloat16).astype(jnp.float32)
        twice = jnp.where(rows == cols, 2.0 * scale, 0.0)
        for i in range(count):
            for j in range(count):
                place = (slice(i * TILE, (i + 1) * TILE), slice(j * TILE, (j + 1) * TILE))
                product = (damped[place].astype(jnp.float32) * factor).astype(jnp.bfloat16)
                moved = product.astype(jnp.float32) * factor
                iterate[place] = (twice - moved) if i == j else -moved

    def sweep(step, carry):
        currents = [iterate[...].astype(jnp.bfloat16) for _, iterate, _ in chains]
        products = [
            jnp.dot(damped[...], current, preferred_element_type=jnp.float32).astype(jnp.bfloat16)
            for (damped, _, _), current in zip(chains, currents)
        ]
        for (_, iterate, _), product, current in zip(chains, products, currents):
            iterate[...] = 2.0 * iterate[...] - jnp.dot(
                product, current, preferred_element_type=jnp.float32
            )
        return carry

    lax.fori_loop(0, ITERS - 1, sweep, 0)
    inverse_in = iterate_in_ref[...].astype(jnp.bfloat16)
    left = jnp.dot(inverse_in, weight_block_ref[...], preferred_element_type=jnp.float32)
    right = iterate_out_ref[:, own_column].astype(jnp.bfloat16)
    result_ref[...] = jnp.dot(
        left.astype(jnp.bfloat16), right, preferred_element_type=jnp.float32
    ).astype(jnp.bfloat16)


VMEM_SPEC = pl.BlockSpec(memory_space=pltpu.VMEM)


def local_call(kernel, name, operands, outs, scratch=(), flops=0):
    multiple = isinstance(outs, tuple)
    listed = outs if multiple else (outs,)
    moved = sum(a.size * a.dtype.itemsize for a in operands + tuple(listed))
    return pl.pallas_call(
        kernel,
        out_shape=outs,
        in_specs=[VMEM_SPEC] * len(operands),
        out_specs=tuple([VMEM_SPEC] * len(listed)) if multiple else VMEM_SPEC,
        scratch_shapes=list(scratch),
        compiler_params=pltpu.CompilerParams(vmem_limit_bytes=VMEM_LIMIT),
        cost_estimate=pl.CostEstimate(flops=flops, bytes_accessed=moved, transcendentals=0),
        name=name,
    )(*operands)


def shape_of(*dims, dtype=jnp.float32):
    return jax.ShapeDtypeStruct(dims, dtype)


def exchange(value, axis, groups=None):
    return lax.all_to_all(value, axis, 0, 0, tiled=True, axis_index_groups=groups)


def swap_core(value):
    pairs = [(place, place ^ 1) for place in range(lax.axis_size("blk"))]
    return lax.ppermute(value, "blk", pairs)


def swap_along(value, stride, step):
    pairs = [(place, place ^ (stride * step)) for place in range(lax.axis_size("blk"))]
    return lax.ppermute(value, "blk", pairs)


def swap_half(value):
    pairs = [(place, place ^ 1) for place in range(lax.axis_size("grp"))]
    return lax.ppermute(value, "grp", pairs)


def shards(activations, output_grads, grad_weight):
    groups = lax.axis_size("grp")
    width = grad_weight.shape[0]
    half = grad_weight.shape[1]
    count = width // TILE
    packed_rows = width * width // (2 * TILE)
    total_tokens = activations.shape[0] * groups
    in_rows = packed_rows // groups
    share_rows = packed_rows // CORES
    piece_rows = share_rows // RING
    y_stride, x_stride = CORES, CORES * RING
    half_type = jnp.bfloat16

    other_grads = swap_half(output_grads)
    send_in = local_call(
        lambda *refs: gram_in_kernel(total_tokens, *refs),
        "gram_in",
        (activations, output_grads),
        shape_of(groups, in_rows + EXTRA, TILE),
        flops=2 * activations.shape[0] * width * width,
    )
    got_in = exchange(send_in, "grp")

    keep, give = local_call(
        lambda *refs: gram_out_kernel(total_tokens, *refs),
        "gram_out",
        (output_grads, other_grads),
        (shape_of(share_rows + EXTRA, TILE),) * 2,
        scratch=[
            pltpu.VMEM((output_grads.shape[0], width), half_type),
            pltpu.VMEM((packed_rows, TILE), jnp.float32),
        ],
        flops=LATE_START * 3,
    )
    keep, *gives = local_call(
        add_cores_kernel,
        "add_cores",
        (keep, swap_core(give)),
        (shape_of(piece_rows + EXTRA, TILE),) * RING,
    )
    taken = [swap_along(give, x_stride, step + 1) for step, give in enumerate(gives)]
    other_weight = swap_half(grad_weight)
    got_in, other_weight = lax.optimization_barrier((got_in, other_weight))
    to_all_in, extra_in, part_y = local_call(
        lambda *refs: sum_both_kernel(count, *refs),
        "sum_both",
        (got_in, keep, *taken),
        (
            shape_of(groups, in_rows, TILE, dtype=half_type),
            shape_of(EXTRA, TILE),
            shape_of(piece_rows + EXTRA, TILE),
        ),
    )
    all_in = exchange(to_all_in, "grp")
    taken = [swap_along(part_y, y_stride, step) for step in range(1, RING)]
    to_all_out, extra_out = local_call(
        lambda *refs: sum_y_kernel(count, *refs),
        "sum_y",
        (part_y, *taken),
        (
            shape_of(RING * CORES, piece_rows + EXTRA_HALF, TILE, dtype=half_type),
            shape_of(EXTRA, TILE),
        ),
        flops=LATE_START,
    )
    same_y = [
        [x * x_stride + y * y_stride + core for x in range(RING) for core in range(CORES)]
        for y in range(RING)
    ]
    all_out = exchange(to_all_out, "blk", same_y)

    block = (width, width)
    damped_in = local_call(unpack_in_kernel, "unpack_in", (all_in,), shape_of(*block, dtype=half_type))
    return local_call(
        invert_kernel,
        "invert",
        (damped_in, all_out, extra_in, extra_out, grad_weight, other_weight),
        shape_of(width, half, dtype=half_type),
        scratch=[
            pltpu.VMEM(block, half_type),
            pltpu.VMEM(block, half_type),
            pltpu.VMEM(block, jnp.float32),
            pltpu.VMEM(block, jnp.float32),
            pltpu.VMEM(block, half_type),
        ],
        flops=2 * (4 * (ITERS - 1) + 2) * width * width * width,
    )


def solution(mesh):
    in_specs = (P("grp", "blk"), P("blk", "grp"), P("blk", "grp"))
    out_specs = P("blk", "grp")
    return jax.shard_map(shards, mesh=mesh, in_specs=in_specs, out_specs=out_specs, check_vma=False)
```

```python
import functools

import jax
import jax.numpy as jnp
from jax import lax
from jax.experimental import pallas as pl
from jax.experimental.pallas import tpu as pltpu
from jax.sharding import PartitionSpec as P

ITERS = 6
DAMP_ROOT = 0.1
TILE = 128
CORES = 2
RING = 4
EXTRA = 8
EXTRA_HALF = 16
LATE_START = 10**10
VMEM_LIMIT = 48 * 1024 * 1024


def tile_plan(count):
    off = [(i, j) for i in range(count) for j in range(i + 1, count)]
    pairs = [(i, i + 1) for i in range(0, count, 2)]
    return off, pairs


def tile_masks():
    rows = lax.broadcasted_iota(jnp.int32, (TILE, TILE), 0)
    cols = lax.broadcasted_iota(jnp.int32, (TILE, TILE), 1)
    return rows, cols


def gram_tiles(left, right, scale):
    return scale * lax.dot_general(
        left, right, (((0,), (0,)), ((), ())), preferred_element_type=jnp.float32
    )


def packed_gram(data_ref, scale, store):
    width = data_ref.shape[1]
    count = width // TILE
    half = width // 2
    low, high = data_ref[:, :half], data_ref[:, half:]
    parts = {
        (0, 0): gram_tiles(low, low, scale),
        (0, 1): gram_tiles(low, high, scale),
        (1, 1): gram_tiles(high, high, scale),
    }
    per = count // 2

    def tile(i, j):
        part = parts[(i // per, j // per)]
        r, c = (i % per) * TILE, (j % per) * TILE
        return part[r : r + TILE, c : c + TILE]

    off, pairs = tile_plan(count)
    rows, cols = tile_masks()
    for position, (i, j) in enumerate(off):
        store(position, tile(i, j))
    for position, (i, j) in enumerate(pairs):
        store(len(off) + position, jnp.where(cols > rows, tile(i, i), tile(j, j)))
    return jnp.concatenate(
        [
            jnp.sum(jnp.where(rows == cols, tile(i, i), 0.0), axis=0, keepdims=True)
            for i in range(count)
        ],
        axis=0,
    )


def unpack_block(fetch, out_ref):
    count = out_ref.shape[0] // TILE
    off, pairs = tile_plan(count)
    rows, cols = tile_masks()

    def put(i, j, value):
        out_ref[i * TILE : (i + 1) * TILE, j * TILE : (j + 1) * TILE] = value.astype(jnp.bfloat16)

    for position, (i, j) in enumerate(off):
        value = fetch(position).astype(jnp.float32)
        put(i, j, value)
        put(j, i, value.T)
    for position, (i, j) in enumerate(pairs):
        value = fetch(len(off) + position).astype(jnp.float32)
        other = value.T
        put(i, i, jnp.where(cols > rows, value, other))
        put(j, j, jnp.where(cols < rows, value, other))


def put_diagonal(diagonal, damping, out_ref):
    rows, cols = tile_masks()
    for i in range(out_ref.shape[0] // TILE):
        place = (slice(i * TILE, (i + 1) * TILE),) * 2
        damped = diagonal[i : i + 1, :] + damping
        tile = out_ref[place].astype(jnp.float32)
        out_ref[place] = jnp.where(rows == cols, damped, tile).astype(jnp.bfloat16)


def total_of(value):
    return jnp.sum(jnp.sum(value, axis=1, keepdims=True), axis=0, keepdims=True)


def gram_in_kernel(tokens, data_ref, grads_ref, out_ref):
    pieces, piece_rows = out_ref.shape[0], out_ref.shape[1] - EXTRA
    per_tile = TILE // piece_rows
    scale = 1.0 / tokens

    def store(position, value):
        for part in range(per_tile):
            out_ref[position * per_tile + part, :piece_rows, :] = value[
                part * piece_rows : (part + 1) * piece_rows
            ]

    diagonal = packed_gram(data_ref, scale, store)
    grads = grads_ref[...].astype(jnp.float32)
    energy = total_of(grads * grads) * scale
    filler = jnp.zeros((EXTRA - diagonal.shape[0] - 1, TILE), jnp.float32)
    extra = jnp.concatenate(
        [diagonal, jnp.broadcast_to(energy, (1, TILE)), filler], axis=0
    )
    for piece in range(pieces):
        out_ref[piece, piece_rows:, :] = extra


def gram_out_kernel(tokens, own_ref, other_ref, keep_ref, send_ref, data_ref, packed_ref):
    half = own_ref.shape[1]
    parity = lax.axis_index("grp") % 2
    core = lax.axis_index("blk") % CORES
    data_ref[:, pl.ds(pl.multiple_of(parity * half, half), half)] = own_ref[...]
    data_ref[:, pl.ds(pl.multiple_of((1 - parity) * half, half), half)] = other_ref[...]

    def store(position, value):
        packed_ref[position * TILE : (position + 1) * TILE, :] = value

    diagonal = packed_gram(data_ref, 1.0 / tokens, store)
    filler = jnp.zeros((EXTRA - diagonal.shape[0], TILE), jnp.float32)
    extra = jnp.concatenate([diagonal, filler], axis=0)
    share = keep_ref.shape[0] - EXTRA
    for ref, owner in ((keep_ref, core), (send_ref, 1 - core)):
        start = pl.multiple_of(owner * share, share)
        ref[:share, :] = packed_ref[pl.ds(start, share), :]
        ref[share:, :] = extra


def along_x():
    return lax.axis_index("blk") // (RING * CORES)


def fold_kernel(bit, left_ref, right_ref, keep_ref, give_ref):
    rows = keep_ref.shape[0] - EXTRA
    extra = left_ref[2 * rows :, :] + right_ref[2 * rows :, :]
    own = (along_x() >> bit) & 1
    for ref, owner in ((keep_ref, own), (give_ref, 1 - own)):
        place = pl.ds(pl.multiple_of(owner * rows, rows), rows)
        ref[:rows, :] = left_ref[place, :] + right_ref[place, :]
        ref[rows:, :] = extra


def add_kernel(left_ref, right_ref, out_ref):
    out_ref[...] = left_ref[...] + right_ref[...]


def sum_pieces(ref):
    total = ref[0]
    for piece in range(1, ref.shape[0]):
        total = total + ref[piece]
    return total


def split_rows(value):
    high = value.astype(jnp.bfloat16).astype(jnp.float32)
    rest = value - high
    middle = rest.astype(jnp.bfloat16).astype(jnp.float32)
    return [high, middle, rest - middle]


def sum_both_kernel(
    count, got_ref, left_ref, right_ref, send_ref, extra_in_ref, out_ref
):
    total = sum_pieces(got_ref)
    rows = send_ref.shape[1]
    rounded = total[:rows].astype(jnp.bfloat16)
    for piece in range(send_ref.shape[0]):
        send_ref[piece] = rounded
    extra = total[rows:]
    extra_in_ref[...] = extra
    total = left_ref[...] + right_ref[...]
    rows = total.shape[0] - EXTRA
    trace_in = jnp.broadcast_to(total_of(extra[:count]), (1, TILE))
    energy_out = extra[count : count + 1]
    filler = jnp.zeros((EXTRA - count - 2, TILE), jnp.float32)
    out_ref[...] = jnp.concatenate(
        [total[: rows + count], trace_in, energy_out, filler], axis=0
    )


def sum_y_kernel(count, left_ref, right_ref, send_ref, extra_ref):
    total = left_ref[...] + right_ref[...]
    rows = total.shape[0] - EXTRA
    extra = total[rows:]
    scalars = split_rows(extra[count : count + 1]) + split_rows(extra[count + 1 : count + 2])
    filler = jnp.zeros((EXTRA_HALF - len(scalars), TILE), jnp.float32)
    block = jnp.concatenate([total[:rows]] + scalars + [filler], axis=0).astype(jnp.bfloat16)
    for piece in range(send_ref.shape[0]):
        send_ref[piece] = block
    extra_ref[...] = extra


def unpack_in_kernel(got_ref, out_ref):
    rows = got_ref.shape[1]
    per_tile = TILE // rows
    unpack_block(
        lambda position: jnp.concatenate(
            [got_ref[position * per_tile + part] for part in range(per_tile)], axis=0
        ),
        out_ref,
    )


def invert_kernel(
    damped_in_ref,
    got_out_ref,
    extra_in_ref,
    extra_out_ref,
    weight_ref,
    other_weight_ref,
    result_ref,
    full_in_ref,
    damped_out_ref,
    iterate_in_ref,
    iterate_out_ref,
    weight_block_ref,
):
    width = damped_in_ref.shape[0]
    count = width // TILE
    half = weight_ref.shape[1]
    parity = lax.axis_index("grp") % 2
    pieces, rows_out = got_out_ref.shape[0], got_out_ref.shape[1] - EXTRA_HALF
    own_column = pl.ds(pl.multiple_of(parity * half, half), half)
    other_column = pl.ds(pl.multiple_of((1 - parity) * half, half), half)
    weight_block_ref[:, own_column] = weight_ref[...]
    weight_block_ref[:, other_column] = other_weight_ref[...]

    scalars = jnp.zeros((EXTRA_HALF, TILE), jnp.float32)
    for piece in range(pieces):
        scalars = scalars + got_out_ref[piece, rows_out:, :].astype(jnp.float32)
    sum_in = scalars[0:1] + scalars[1:2] + scalars[2:3]
    sum_out = scalars[3:4] + scalars[4:5] + scalars[5:6]
    owners = lax.axis_size("blk")
    blocks_out = lax.axis_size("grp") // 2
    pi_ratio = jnp.sqrt((sum_in / (owners * width)) / (sum_out / (blocks_out * width)))
    damping_in = DAMP_ROOT * pi_ratio
    damping_out = DAMP_ROOT / pi_ratio
    diagonal_in = extra_in_ref[:count, :]
    diagonal_out = extra_out_ref[:count, :]
    scale_in = 1.0 / (total_of(diagonal_in) + width * damping_in)
    scale_out = 1.0 / (total_of(diagonal_out) + width * damping_out)

    full_in_ref[...] = damped_in_ref[...]
    put_diagonal(diagonal_in, damping_in, full_in_ref)
    unpack_block(
        lambda position: got_out_ref[
            position % RING * CORES + position // RING, :rows_out, :
        ],
        damped_out_ref,
    )
    put_diagonal(diagonal_out, damping_out, damped_out_ref)

    chains = (
        (full_in_ref, iterate_in_ref, scale_in),
        (damped_out_ref, iterate_out_ref, scale_out),
    )
    rows, cols = tile_masks()
    for damped, iterate, scale in chains:
        factor = scale.astype(jnp.bfloat16).astype(jnp.float32)
        twice = jnp.where(rows == cols, 2.0 * scale, 0.0)
        for i in range(count):
            for j in range(count):
                place = (slice(i * TILE, (i + 1) * TILE), slice(j * TILE, (j + 1) * TILE))
                product = (damped[place].astype(jnp.float32) * factor).astype(jnp.bfloat16)
                moved = product.astype(jnp.float32) * factor
                iterate[place] = (twice - moved) if i == j else -moved

    def sweep(step, carry):
        currents = [iterate[...].astype(jnp.bfloat16) for _, iterate, _ in chains]
        products = [
            jnp.dot(damped[...], current, preferred_element_type=jnp.float32).astype(jnp.bfloat16)
            for (damped, _, _), current in zip(chains, currents)
        ]
        for (_, iterate, _), product, current in zip(chains, products, currents):
            iterate[...] = 2.0 * iterate[...] - jnp.dot(
                product, current, preferred_element_type=jnp.float32
            )
        return carry

    lax.fori_loop(0, ITERS - 1, sweep, 0)
    inverse_in = iterate_in_ref[...].astype(jnp.bfloat16)
    left = jnp.dot(inverse_in, weight_block_ref[...], preferred_element_type=jnp.float32)
    right = iterate_out_ref[:, own_column].astype(jnp.bfloat16)
    result_ref[...] = jnp.dot(
        left.astype(jnp.bfloat16), right, preferred_element_type=jnp.float32
    ).astype(jnp.bfloat16)


VMEM_SPEC = pl.BlockSpec(memory_space=pltpu.VMEM)


def local_call(kernel, name, operands, outs, scratch=(), flops=0):
    multiple = isinstance(outs, tuple)
    listed = outs if multiple else (outs,)
    moved = sum(a.size * a.dtype.itemsize for a in operands + tuple(listed))
    return pl.pallas_call(
        kernel,
        out_shape=outs,
        in_specs=[VMEM_SPEC] * len(operands),
        out_specs=tuple([VMEM_SPEC] * len(listed)) if multiple else VMEM_SPEC,
        scratch_shapes=list(scratch),
        compiler_params=pltpu.CompilerParams(vmem_limit_bytes=VMEM_LIMIT),
        cost_estimate=pl.CostEstimate(flops=flops, bytes_accessed=moved, transcendentals=0),
        name=name,
    )(*operands)


def shape_of(*dims, dtype=jnp.float32):
    return jax.ShapeDtypeStruct(dims, dtype)


def exchange(value, axis, groups=None):
    return lax.all_to_all(value, axis, 0, 0, tiled=True, axis_index_groups=groups)


def swap_core(value):
    pairs = [(place, place ^ 1) for place in range(lax.axis_size("blk"))]
    return lax.ppermute(value, "blk", pairs)


def swap_along(value, stride, step):
    pairs = [(place, place ^ (stride * step)) for place in range(lax.axis_size("blk"))]
    return lax.ppermute(value, "blk", pairs)


def swap_half(value):
    pairs = [(place, place ^ 1) for place in range(lax.axis_size("grp"))]
    return lax.ppermute(value, "grp", pairs)


def shards(activations, output_grads, grad_weight):
    groups = lax.axis_size("grp")
    width = grad_weight.shape[0]
    half = grad_weight.shape[1]
    count = width // TILE
    packed_rows = width * width // (2 * TILE)
    total_tokens = activations.shape[0] * groups
    in_rows = packed_rows // groups
    share_rows = packed_rows // CORES
    piece_rows = share_rows // RING
    y_stride, x_stride = CORES, CORES * RING
    half_type = jnp.bfloat16

    other_grads = swap_half(output_grads)
    send_in = local_call(
        functools.partial(gram_in_kernel, total_tokens),
        "gram_in",
        (activations, output_grads),
        shape_of(groups, in_rows + EXTRA, TILE),
        flops=2 * activations.shape[0] * width * width,
    )
    got_in = exchange(send_in, "grp")

    keep, give = local_call(
        functools.partial(gram_out_kernel, total_tokens),
        "gram_out",
        (output_grads, other_grads),
        (shape_of(share_rows + EXTRA, TILE),) * 2,
        scratch=[
            pltpu.VMEM((output_grads.shape[0], width), half_type),
            pltpu.VMEM((packed_rows, TILE), jnp.float32),
        ],
        flops=LATE_START * 3,
    )
    folds = (
        ("fold_cores", 1, share_rows // 2, swap_core),
        ("fold_x", 0, piece_rows, lambda value: swap_along(value, x_stride, 3)),
    )
    for name, bit, rows, swap in folds:
        keep, give = local_call(
            functools.partial(fold_kernel, bit),
            name,
            (keep, swap(give)),
            (shape_of(rows + EXTRA, TILE),) * 2,
        )
    to_all_in, extra_in, part_y = local_call(
        functools.partial(sum_both_kernel, count),
        "sum_both",
        (got_in, keep, swap_along(give, x_stride, 1)),
        (
            shape_of(groups, in_rows, TILE, dtype=half_type),
            shape_of(EXTRA, TILE),
            shape_of(piece_rows + EXTRA, TILE),
        ),
    )
    all_in = exchange(to_all_in, "grp")
    part_y = local_call(
        add_kernel,
        "add_y",
        (part_y, swap_along(part_y, y_stride, 1)),
        shape_of(*part_y.shape),
        flops=LATE_START,
    )
    to_all_out, extra_out = local_call(
        functools.partial(sum_y_kernel, count),
        "sum_y",
        (part_y, swap_along(part_y, y_stride, 3)),
        (
            shape_of(RING * CORES, piece_rows + EXTRA_HALF, TILE, dtype=half_type),
            shape_of(EXTRA, TILE),
        ),
    )
    same_y = [
        [x * x_stride + y * y_stride + core for x in range(RING) for core in range(CORES)]
        for y in range(RING)
    ]
    sent_weight, to_all_out = lax.optimization_barrier((grad_weight, to_all_out))
    other_weight = swap_half(sent_weight)
    all_out = exchange(to_all_out, "blk", same_y)

    block = (width, width)
    damped_in = local_call(unpack_in_kernel, "unpack_in", (all_in,), shape_of(*block, dtype=half_type))
    return local_call(
        invert_kernel,
        "invert",
        (damped_in, all_out, extra_in, extra_out, grad_weight, other_weight),
        shape_of(width, half, dtype=half_type),
        scratch=[
            pltpu.VMEM(block, half_type),
            pltpu.VMEM(block, half_type),
            pltpu.VMEM(block, jnp.float32),
            pltpu.VMEM(block, jnp.float32),
            pltpu.VMEM(block, half_type),
        ],
        flops=2 * (4 * (ITERS - 1) + 2) * width * width * width,
    )


def solution(mesh):
    in_specs = (P("grp", "blk"), P("blk", "grp"), P("blk", "grp"))
    out_specs = P("blk", "grp")
    return jax.shard_map(shards, mesh=mesh, in_specs=in_specs, out_specs=out_specs, check_vma=False)
```

```python
import functools

import jax
import jax.numpy as jnp
from jax import lax
from jax.experimental import pallas as pl
from jax.experimental.pallas import tpu as pltpu
from jax.sharding import PartitionSpec as P

ITERS = 6
DAMP_ROOT = 0.1
TILE = 128
CORES = 2
CHUNKS = 4
RING = 4
EXTRA = 8
EXTRA_HALF = 16
LATE_START = 10**10
VMEM_LIMIT = 48 * 1024 * 1024


def tile_plan(count):
    off = [(i, j) for i in range(count) for j in range(i + 1, count)]
    pairs = [(i, i + 1) for i in range(0, count, 2)]
    return off, pairs


def tile_masks():
    rows = lax.broadcasted_iota(jnp.int32, (TILE, TILE), 0)
    cols = lax.broadcasted_iota(jnp.int32, (TILE, TILE), 1)
    return rows, cols


def gram_parts(data):
    half = data.shape[1] // 2
    low, high = data[:, :half], data[:, half:]
    return [
        lax.dot_general(left, right, (((0,), (0,)), ((), ())), preferred_element_type=jnp.float32)
        for left, right in ((low, low), (low, high), (high, high))
    ]


def pack_gram(quarters, store):
    per = quarters[0].shape[0] // TILE
    count = 2 * per

    def tile(i, j):
        part = quarters[i // per + j // per]
        r, c = (i % per) * TILE, (j % per) * TILE
        return part[r : r + TILE, c : c + TILE]

    off, pairs = tile_plan(count)
    rows, cols = tile_masks()
    for position, (i, j) in enumerate(off):
        store(position, tile(i, j))
    for position, (i, j) in enumerate(pairs):
        store(len(off) + position, jnp.where(cols > rows, tile(i, i), tile(j, j)))
    return jnp.concatenate(
        [
            jnp.sum(jnp.where(rows == cols, tile(i, i), 0.0), axis=0, keepdims=True)
            for i in range(count)
        ],
        axis=0,
    )


def unpack_block(fetch, out_ref):
    count = out_ref.shape[0] // TILE
    off, pairs = tile_plan(count)
    rows, cols = tile_masks()

    def put(i, j, value):
        out_ref[i * TILE : (i + 1) * TILE, j * TILE : (j + 1) * TILE] = value.astype(jnp.bfloat16)

    for position, (i, j) in enumerate(off):
        value = fetch(position).astype(jnp.float32)
        put(i, j, value)
        put(j, i, value.T)
    for position, (i, j) in enumerate(pairs):
        value = fetch(len(off) + position).astype(jnp.float32)
        other = value.T
        put(i, i, jnp.where(cols > rows, value, other))
        put(j, j, jnp.where(cols < rows, value, other))


def put_diagonal(diagonal, damping, out_ref):
    rows, cols = tile_masks()
    for i in range(out_ref.shape[0] // TILE):
        place = (slice(i * TILE, (i + 1) * TILE),) * 2
        damped = diagonal[i : i + 1, :] + damping
        tile = out_ref[place].astype(jnp.float32)
        out_ref[place] = jnp.where(rows == cols, damped, tile).astype(jnp.bfloat16)


def total_of(value):
    return jnp.sum(jnp.sum(value, axis=1, keepdims=True), axis=0, keepdims=True)


def gram_in_kernel(tokens, data_hbm, grads_hbm, out_ref, data_ref, grads_ref, parts_ref, sems):
    pieces, piece_rows = out_ref.shape[0], out_ref.shape[1] - EXTRA
    per_tile = TILE // piece_rows
    scale = 1.0 / tokens
    rows = data_ref.shape[0] // CHUNKS
    copies = []
    for chunk in range(CHUNKS):
        place = pl.ds(chunk * rows, rows)
        copies.append(
            pltpu.make_async_copy(data_hbm.at[place], data_ref.at[place], sems.at[chunk])
        )
    copies.append(pltpu.make_async_copy(grads_hbm, grads_ref, sems.at[CHUNKS]))
    for copy in copies:
        copy.start()
    for chunk in range(CHUNKS):
        copies[chunk].wait()
        part = gram_parts(data_ref[chunk * rows : (chunk + 1) * rows, :])
        for position, value in enumerate(part):
            parts_ref[position] = value if chunk == 0 else parts_ref[position] + value
    copies[CHUNKS].wait()

    def store(position, value):
        for part in range(per_tile):
            out_ref[position * per_tile + part, :piece_rows, :] = value[
                part * piece_rows : (part + 1) * piece_rows
            ]

    diagonal = pack_gram([scale * parts_ref[position] for position in range(3)], store)
    grads = grads_ref[...].astype(jnp.float32)
    energy = total_of(grads * grads) * scale
    filler = jnp.zeros((EXTRA - diagonal.shape[0] - 1, TILE), jnp.float32)
    extra = jnp.concatenate(
        [diagonal, jnp.broadcast_to(energy, (1, TILE)), filler], axis=0
    )
    for piece in range(pieces):
        out_ref[piece, piece_rows:, :] = extra


def gram_out_kernel(tokens, own_ref, other_ref, keep_ref, send_ref, data_ref, packed_ref):
    half = own_ref.shape[1]
    parity = lax.axis_index("grp") % 2
    core = lax.axis_index("blk") % CORES
    data_ref[:, pl.ds(pl.multiple_of(parity * half, half), half)] = own_ref[...]
    data_ref[:, pl.ds(pl.multiple_of((1 - parity) * half, half), half)] = other_ref[...]

    def store(position, value):
        packed_ref[position * TILE : (position + 1) * TILE, :] = value

    scale = 1.0 / tokens
    diagonal = pack_gram([scale * part for part in gram_parts(data_ref[...])], store)
    filler = jnp.zeros((EXTRA - diagonal.shape[0], TILE), jnp.float32)
    extra = jnp.concatenate([diagonal, filler], axis=0)
    share = keep_ref.shape[0] - EXTRA
    for ref, owner in ((keep_ref, core), (send_ref, 1 - core)):
        start = pl.multiple_of(owner * share, share)
        ref[:share, :] = packed_ref[pl.ds(start, share), :]
        ref[share:, :] = extra


def along_x():
    return lax.axis_index("blk") // (RING * CORES)


def fold_kernel(bit, left_ref, right_ref, keep_ref, give_ref):
    rows = keep_ref.shape[0] - EXTRA
    extra = left_ref[2 * rows :, :] + right_ref[2 * rows :, :]
    own = (along_x() >> bit) & 1
    for ref, owner in ((keep_ref, own), (give_ref, 1 - own)):
        place = pl.ds(pl.multiple_of(owner * rows, rows), rows)
        ref[:rows, :] = left_ref[place, :] + right_ref[place, :]
        ref[rows:, :] = extra


def stage_kernel(after_ref, value_ref, out_ref):
    out_ref[...] = value_ref[...]


def add_kernel(left_ref, right_ref, out_ref):
    out_ref[...] = left_ref[...] + right_ref[...]


def sum_pieces(ref):
    total = ref[0]
    for piece in range(1, ref.shape[0]):
        total = total + ref[piece]
    return total


def split_rows(value):
    high = value.astype(jnp.bfloat16).astype(jnp.float32)
    rest = value - high
    middle = rest.astype(jnp.bfloat16).astype(jnp.float32)
    return [high, middle, rest - middle]


def sum_both_kernel(
    count, got_ref, left_ref, right_ref, send_ref, extra_in_ref, out_ref
):
    total = sum_pieces(got_ref)
    rows = send_ref.shape[1]
    rounded = total[:rows].astype(jnp.bfloat16)
    for piece in range(send_ref.shape[0]):
        send_ref[piece] = rounded
    extra = total[rows:]
    extra_in_ref[...] = extra
    total = left_ref[...] + right_ref[...]
    rows = total.shape[0] - EXTRA
    trace_in = jnp.broadcast_to(total_of(extra[:count]), (1, TILE))
    energy_out = extra[count : count + 1]
    filler = jnp.zeros((EXTRA - count - 2, TILE), jnp.float32)
    out_ref[...] = jnp.concatenate(
        [total[: rows + count], trace_in, energy_out, filler], axis=0
    )


def sum_y_kernel(count, left_ref, right_ref, send_ref, extra_ref):
    total = left_ref[...] + right_ref[...]
    rows = total.shape[0] - EXTRA
    extra = total[rows:]
    scalars = split_rows(extra[count : count + 1]) + split_rows(extra[count + 1 : count + 2])
    filler = jnp.zeros((EXTRA_HALF - len(scalars), TILE), jnp.float32)
    block = jnp.concatenate([total[:rows]] + scalars + [filler], axis=0).astype(jnp.bfloat16)
    for piece in range(send_ref.shape[0]):
        send_ref[piece] = block
    extra_ref[...] = extra


def unpack_in_kernel(got_ref, out_ref):
    rows = got_ref.shape[1]
    per_tile = TILE // rows
    unpack_block(
        lambda position: jnp.concatenate(
            [got_ref[position * per_tile + part] for part in range(per_tile)], axis=0
        ),
        out_ref,
    )


def invert_kernel(
    damped_in_ref,
    got_out_ref,
    extra_in_ref,
    extra_out_ref,
    weight_ref,
    other_weight_ref,
    result_ref,
    full_in_ref,
    damped_out_ref,
    iterate_in_ref,
    iterate_out_ref,
    weight_block_ref,
):
    width = damped_in_ref.shape[0]
    count = width // TILE
    half = weight_ref.shape[1]
    parity = lax.axis_index("grp") % 2
    pieces, rows_out = got_out_ref.shape[0], got_out_ref.shape[1] - EXTRA_HALF
    own_column = pl.ds(pl.multiple_of(parity * half, half), half)
    other_column = pl.ds(pl.multiple_of((1 - parity) * half, half), half)
    weight_block_ref[:, own_column] = weight_ref[...]
    weight_block_ref[:, other_column] = other_weight_ref[...]

    scalars = jnp.zeros((EXTRA_HALF, TILE), jnp.float32)
    for piece in range(pieces):
        scalars = scalars + got_out_ref[piece, rows_out:, :].astype(jnp.float32)
    sum_in = scalars[0:1] + scalars[1:2] + scalars[2:3]
    sum_out = scalars[3:4] + scalars[4:5] + scalars[5:6]
    owners = lax.axis_size("blk")
    blocks_out = lax.axis_size("grp") // 2
    pi_ratio = jnp.sqrt((sum_in / (owners * width)) / (sum_out / (blocks_out * width)))
    damping_in = DAMP_ROOT * pi_ratio
    damping_out = DAMP_ROOT / pi_ratio
    diagonal_in = extra_in_ref[:count, :]
    diagonal_out = extra_out_ref[:count, :]
    scale_in = 1.0 / (total_of(diagonal_in) + width * damping_in)
    scale_out = 1.0 / (total_of(diagonal_out) + width * damping_out)

    full_in_ref[...] = damped_in_ref[...]
    put_diagonal(diagonal_in, damping_in, full_in_ref)
    unpack_block(
        lambda position: got_out_ref[
            position % RING * CORES + position // RING, :rows_out, :
        ],
        damped_out_ref,
    )
    put_diagonal(diagonal_out, damping_out, damped_out_ref)

    chains = (
        (full_in_ref, iterate_in_ref, scale_in),
        (damped_out_ref, iterate_out_ref, scale_out),
    )
    rows, cols = tile_masks()
    for damped, iterate, scale in chains:
        factor = scale.astype(jnp.bfloat16).astype(jnp.float32)
        twice = jnp.where(rows == cols, 2.0 * scale, 0.0)
        for i in range(count):
            for j in range(count):
                place = (slice(i * TILE, (i + 1) * TILE), slice(j * TILE, (j + 1) * TILE))
                product = (damped[place].astype(jnp.float32) * factor).astype(jnp.bfloat16)
                moved = product.astype(jnp.float32) * factor
                iterate[place] = (twice - moved) if i == j else -moved

    for _ in range(ITERS - 1):
        currents = [iterate[...].astype(jnp.bfloat16) for _, iterate, _ in chains]
        products = [
            jnp.dot(damped[...], current, preferred_element_type=jnp.float32).astype(jnp.bfloat16)
            for (damped, _, _), current in zip(chains, currents)
        ]
        for (_, iterate, _), product, current in zip(chains, products, currents):
            iterate[...] = 2.0 * iterate[...] - jnp.dot(
                product, current, preferred_element_type=jnp.float32
            )
    inverse_in = iterate_in_ref[...].astype(jnp.bfloat16)
    left = jnp.dot(inverse_in, weight_block_ref[...], preferred_element_type=jnp.float32)
    right = iterate_out_ref[:, own_column].astype(jnp.bfloat16)
    result_ref[...] = jnp.dot(
        left.astype(jnp.bfloat16), right, preferred_element_type=jnp.float32
    ).astype(jnp.bfloat16)


VMEM_SPEC = pl.BlockSpec(memory_space=pltpu.VMEM)


def local_call(kernel, name, operands, outs, scratch=(), flops=0, space=pltpu.VMEM):
    multiple = isinstance(outs, tuple)
    listed = outs if multiple else (outs,)
    moved = sum(a.size * a.dtype.itemsize for a in operands + tuple(listed))
    return pl.pallas_call(
        kernel,
        out_shape=outs,
        in_specs=[pl.BlockSpec(memory_space=space)] * len(operands),
        out_specs=tuple([VMEM_SPEC] * len(listed)) if multiple else VMEM_SPEC,
        scratch_shapes=list(scratch),
        compiler_params=pltpu.CompilerParams(vmem_limit_bytes=VMEM_LIMIT),
        cost_estimate=pl.CostEstimate(flops=flops, bytes_accessed=moved, transcendentals=0),
        name=name,
    )(*operands)


def shape_of(*dims, dtype=jnp.float32):
    return jax.ShapeDtypeStruct(dims, dtype)


def exchange(value, axis, groups=None):
    return lax.all_to_all(value, axis, 0, 0, tiled=True, axis_index_groups=groups)


def swap_core(value):
    pairs = [(place, place ^ 1) for place in range(lax.axis_size("blk"))]
    return lax.ppermute(value, "blk", pairs)


def swap_along(value, stride, step):
    pairs = [(place, place ^ (stride * step)) for place in range(lax.axis_size("blk"))]
    return lax.ppermute(value, "blk", pairs)


def swap_half(value):
    pairs = [(place, place ^ 1) for place in range(lax.axis_size("grp"))]
    return lax.ppermute(value, "grp", pairs)


def shards(activations, output_grads, grad_weight):
    groups = lax.axis_size("grp")
    width = grad_weight.shape[0]
    half = grad_weight.shape[1]
    count = width // TILE
    packed_rows = width * width // (2 * TILE)
    total_tokens = activations.shape[0] * groups
    in_rows = packed_rows // groups
    share_rows = packed_rows // CORES
    piece_rows = share_rows // RING
    y_stride, x_stride = CORES, CORES * RING
    half_type = jnp.bfloat16

    other_grads = swap_half(output_grads)
    send_in = local_call(
        functools.partial(gram_in_kernel, total_tokens),
        "gram_in",
        (activations, output_grads),
        shape_of(groups, in_rows + EXTRA, TILE),
        scratch=[
            pltpu.VMEM(activations.shape, half_type),
            pltpu.VMEM(output_grads.shape, half_type),
            pltpu.VMEM((3, width // 2, width // 2), jnp.float32),
            pltpu.SemaphoreType.DMA((CHUNKS + 1,)),
        ],
        flops=2 * activations.shape[0] * width * width,
        space=pl.ANY,
    )
    got_in = exchange(send_in, "grp")

    keep, give = local_call(
        functools.partial(gram_out_kernel, total_tokens),
        "gram_out",
        (output_grads, other_grads),
        (shape_of(share_rows + EXTRA, TILE),) * 2,
        scratch=[
            pltpu.VMEM((output_grads.shape[0], width), half_type),
            pltpu.VMEM((packed_rows, TILE), jnp.float32),
        ],
        flops=LATE_START * 3,
    )
    folds = (
        ("fold_cores", 1, share_rows // 2, swap_core),
        ("fold_x", 0, piece_rows, lambda value: swap_along(value, x_stride, 3)),
    )
    for name, bit, rows, swap in folds:
        keep, give = local_call(
            functools.partial(fold_kernel, bit),
            name,
            (keep, swap(give)),
            (shape_of(rows + EXTRA, TILE),) * 2,
        )
    sent_weight = local_call(
        stage_kernel,
        "stage_weight",
        (keep, grad_weight),
        shape_of(*grad_weight.shape, dtype=half_type),
        flops=LATE_START,
    )
    other_weight = swap_half(sent_weight)
    to_all_in, extra_in, part_y = local_call(
        functools.partial(sum_both_kernel, count),
        "sum_both",
        (got_in, keep, swap_along(give, x_stride, 1)),
        (
            shape_of(groups, in_rows, TILE, dtype=half_type),
            shape_of(EXTRA, TILE),
            shape_of(piece_rows + EXTRA, TILE),
        ),
    )
    all_in = exchange(to_all_in, "grp")
    part_y = local_call(
        add_kernel,
        "add_y",
        (part_y, swap_along(part_y, y_stride, 1)),
        shape_of(*part_y.shape),
        flops=LATE_START,
    )
    to_all_out, extra_out = local_call(
        functools.partial(sum_y_kernel, count),
        "sum_y",
        (part_y, swap_along(part_y, y_stride, 3)),
        (
            shape_of(RING * CORES, piece_rows + EXTRA_HALF, TILE, dtype=half_type),
            shape_of(EXTRA, TILE),
        ),
    )
    same_y = [
        [x * x_stride + y * y_stride + core for x in range(RING) for core in range(CORES)]
        for y in range(RING)
    ]
    all_out = exchange(to_all_out, "blk", same_y)

    block = (width, width)
    damped_in = local_call(unpack_in_kernel, "unpack_in", (all_in,), shape_of(*block, dtype=half_type), flops=LATE_START)
    return local_call(
        invert_kernel,
        "invert",
        (damped_in, all_out, extra_in, extra_out, grad_weight, other_weight),
        shape_of(width, half, dtype=half_type),
        scratch=[
            pltpu.VMEM(block, half_type),
            pltpu.VMEM(block, half_type),
            pltpu.VMEM(block, jnp.float32),
            pltpu.VMEM(block, jnp.float32),
            pltpu.VMEM(block, half_type),
        ],
        flops=2 * (4 * (ITERS - 1) + 2) * width * width * width,
    )


def solution(mesh):
    in_specs = (P("grp", "blk"), P("blk", "grp"), P("blk", "grp"))
    out_specs = P("blk", "grp")
    return jax.shard_map(shards, mesh=mesh, in_specs=in_specs, out_specs=out_specs, check_vma=False)
```

```python
import functools

import jax
import jax.numpy as jnp
from jax import lax
from jax.experimental import pallas as pl
from jax.experimental.pallas import tpu as pltpu
from jax.sharding import PartitionSpec as P

ITERS = 6
DAMP_ROOT = 0.1
TILE = 128
CORES = 2
CHUNKS = 2
RING = 4
EXTRA = 8
EXTRA_HALF = 16
LATE_START = 10**10
VMEM_LIMIT = 48 * 1024 * 1024
GRAM_LIMIT = 58 * 1024 * 1024


def tile_plan(count):
    off = [(i, j) for i in range(count) for j in range(i + 1, count)]
    pairs = [(i, i + 1) for i in range(0, count, 2)]
    return off, pairs


def tile_masks():
    rows = lax.broadcasted_iota(jnp.int32, (TILE, TILE), 0)
    cols = lax.broadcasted_iota(jnp.int32, (TILE, TILE), 1)
    return rows, cols


def gram_parts(data):
    half = data.shape[1] // 2
    low, high = data[:, :half], data[:, half:]
    return [
        lax.dot_general(left, right, (((0,), (0,)), ((), ())), preferred_element_type=jnp.float32)
        for left, right in ((low, low), (low, high), (high, high))
    ]


def pack_gram(quarters, store):
    per = quarters[0].shape[0] // TILE
    count = 2 * per

    def tile(i, j):
        part = quarters[i // per + j // per]
        r, c = (i % per) * TILE, (j % per) * TILE
        return part[r : r + TILE, c : c + TILE]

    off, pairs = tile_plan(count)
    rows, cols = tile_masks()
    for position, (i, j) in enumerate(off):
        store(position, tile(i, j))
    for position, (i, j) in enumerate(pairs):
        store(len(off) + position, jnp.where(cols > rows, tile(i, i), tile(j, j)))
    return jnp.concatenate(
        [
            jnp.sum(jnp.where(rows == cols, tile(i, i), 0.0), axis=0, keepdims=True)
            for i in range(count)
        ],
        axis=0,
    )


def unpack_block(fetch, out_ref):
    count = out_ref.shape[0] // TILE
    off, pairs = tile_plan(count)
    rows, cols = tile_masks()

    def put(i, j, value):
        out_ref[i * TILE : (i + 1) * TILE, j * TILE : (j + 1) * TILE] = value.astype(jnp.bfloat16)

    for position, (i, j) in enumerate(off):
        value = fetch(position).astype(jnp.float32)
        put(i, j, value)
        put(j, i, value.T)
    for position, (i, j) in enumerate(pairs):
        value = fetch(len(off) + position).astype(jnp.float32)
        other = value.T
        put(i, i, jnp.where(cols > rows, value, other))
        put(j, j, jnp.where(cols < rows, value, other))


def put_diagonal(diagonal, damping, out_ref):
    rows, cols = tile_masks()
    for i in range(out_ref.shape[0] // TILE):
        place = (slice(i * TILE, (i + 1) * TILE),) * 2
        damped = diagonal[i : i + 1, :] + damping
        tile = out_ref[place].astype(jnp.float32)
        out_ref[place] = jnp.where(rows == cols, damped, tile).astype(jnp.bfloat16)


def total_of(value):
    return jnp.sum(jnp.sum(value, axis=1, keepdims=True), axis=0, keepdims=True)


def gram_in_kernel(tokens, data_hbm, grads_hbm, out_ref, data_ref, grads_ref, sems):
    pieces, piece_rows = out_ref.shape[0], out_ref.shape[1] - EXTRA
    per_tile = TILE // piece_rows
    scale = 1.0 / tokens
    rows = data_ref.shape[0] // CHUNKS
    copies = []
    for chunk in range(CHUNKS):
        place = pl.ds(chunk * rows, rows)
        copies.append(
            pltpu.make_async_copy(data_hbm.at[place], data_ref.at[place], sems.at[chunk])
        )
    copies.append(pltpu.make_async_copy(grads_hbm, grads_ref, sems.at[CHUNKS]))
    for copy in reversed(copies):
        copy.start()
    copies[CHUNKS].wait()
    grads = grads_ref[...].astype(jnp.float32)
    energy = total_of(grads * grads) * scale
    for chunk in range(CHUNKS):
        copies[chunk].wait()
        part = gram_parts(data_ref[chunk * rows : (chunk + 1) * rows, :])
        quarters = part if chunk == 0 else [old + new for old, new in zip(quarters, part)]

    def store(position, value):
        for part in range(per_tile):
            out_ref[position * per_tile + part, :piece_rows, :] = value[
                part * piece_rows : (part + 1) * piece_rows
            ]

    diagonal = pack_gram([scale * quarter for quarter in quarters], store)
    filler = jnp.zeros((EXTRA - diagonal.shape[0] - 1, TILE), jnp.float32)
    extra = jnp.concatenate(
        [diagonal, jnp.broadcast_to(energy, (1, TILE)), filler], axis=0
    )
    for piece in range(pieces):
        out_ref[piece, piece_rows:, :] = extra


def gram_out_kernel(tokens, own_ref, other_ref, keep_ref, send_ref, data_ref, packed_ref):
    half = own_ref.shape[1]
    parity = lax.axis_index("grp") % 2
    core = lax.axis_index("blk") % CORES
    data_ref[:, pl.ds(pl.multiple_of(parity * half, half), half)] = own_ref[...]
    data_ref[:, pl.ds(pl.multiple_of((1 - parity) * half, half), half)] = other_ref[...]

    def store(position, value):
        packed_ref[position * TILE : (position + 1) * TILE, :] = value

    scale = 1.0 / tokens
    diagonal = pack_gram([scale * part for part in gram_parts(data_ref[...])], store)
    filler = jnp.zeros((EXTRA - diagonal.shape[0], TILE), jnp.float32)
    extra = jnp.concatenate([diagonal, filler], axis=0)
    share = keep_ref.shape[0] - EXTRA
    for ref, owner in ((keep_ref, core), (send_ref, 1 - core)):
        start = pl.multiple_of(owner * share, share)
        ref[:share, :] = packed_ref[pl.ds(start, share), :]
        ref[share:, :] = extra


def along_x():
    return lax.axis_index("blk") // (RING * CORES)


def fold_kernel(bit, left_ref, right_ref, keep_ref, give_ref):
    rows = keep_ref.shape[0] - EXTRA
    extra = left_ref[2 * rows :, :] + right_ref[2 * rows :, :]
    own = (along_x() >> bit) & 1
    for ref, owner in ((keep_ref, own), (give_ref, 1 - own)):
        place = pl.ds(pl.multiple_of(owner * rows, rows), rows)
        ref[:rows, :] = left_ref[place, :] + right_ref[place, :]
        ref[rows:, :] = extra


def stage_kernel(after_ref, value_ref, out_ref):
    out_ref[...] = value_ref[...]


def add_kernel(left_ref, right_ref, out_ref):
    out_ref[...] = left_ref[...] + right_ref[...]


def sum_pieces(ref):
    total = ref[0]
    for piece in range(1, ref.shape[0]):
        total = total + ref[piece]
    return total


def split_rows(value):
    high = value.astype(jnp.bfloat16).astype(jnp.float32)
    rest = value - high
    middle = rest.astype(jnp.bfloat16).astype(jnp.float32)
    return [high, middle, rest - middle]


def sum_both_kernel(
    count, got_ref, left_ref, right_ref, send_ref, extra_in_ref, out_ref
):
    total = sum_pieces(got_ref)
    rows = send_ref.shape[1]
    rounded = total[:rows].astype(jnp.bfloat16)
    for piece in range(send_ref.shape[0]):
        send_ref[piece] = rounded
    extra = total[rows:]
    extra_in_ref[...] = extra
    total = left_ref[...] + right_ref[...]
    rows = total.shape[0] - EXTRA
    trace_in = jnp.broadcast_to(total_of(extra[:count]), (1, TILE))
    energy_out = extra[count : count + 1]
    filler = jnp.zeros((EXTRA - count - 2, TILE), jnp.float32)
    out_ref[...] = jnp.concatenate(
        [total[: rows + count], trace_in, energy_out, filler], axis=0
    )


def sum_y_kernel(count, left_ref, right_ref, send_ref, extra_ref):
    total = left_ref[...] + right_ref[...]
    rows = total.shape[0] - EXTRA
    extra = total[rows:]
    scalars = split_rows(extra[count : count + 1]) + split_rows(extra[count + 1 : count + 2])
    filler = jnp.zeros((EXTRA_HALF - len(scalars), TILE), jnp.float32)
    block = jnp.concatenate([total[:rows]] + scalars + [filler], axis=0).astype(jnp.bfloat16)
    for piece in range(send_ref.shape[0]):
        send_ref[piece] = block
    extra_ref[...] = extra


def unpack_in_kernel(got_ref, weight_ref, out_ref, sent_ref):
    sent_ref[...] = weight_ref[...]
    rows = got_ref.shape[1]
    per_tile = TILE // rows
    unpack_block(
        lambda position: jnp.concatenate(
            [got_ref[position * per_tile + part] for part in range(per_tile)], axis=0
        ),
        out_ref,
    )


def invert_kernel(
    damped_in_ref,
    got_out_ref,
    extra_in_ref,
    extra_out_ref,
    inverse_ref,
    right_ref,
    full_in_ref,
    damped_out_ref,
    iterate_in_ref,
    iterate_out_ref,
):
    width = damped_in_ref.shape[0]
    count = width // TILE
    half = right_ref.shape[1]
    parity = lax.axis_index("grp") % 2
    pieces, rows_out = got_out_ref.shape[0], got_out_ref.shape[1] - EXTRA_HALF
    own_column = pl.ds(pl.multiple_of(parity * half, half), half)

    scalars = jnp.zeros((EXTRA_HALF, TILE), jnp.float32)
    for piece in range(pieces):
        scalars = scalars + got_out_ref[piece, rows_out:, :].astype(jnp.float32)
    sum_in = scalars[0:1] + scalars[1:2] + scalars[2:3]
    sum_out = scalars[3:4] + scalars[4:5] + scalars[5:6]
    owners = lax.axis_size("blk")
    blocks_out = lax.axis_size("grp") // 2
    pi_ratio = jnp.sqrt((sum_in / (owners * width)) / (sum_out / (blocks_out * width)))
    damping_in = DAMP_ROOT * pi_ratio
    damping_out = DAMP_ROOT / pi_ratio
    diagonal_in = extra_in_ref[:count, :]
    diagonal_out = extra_out_ref[:count, :]
    scale_in = 1.0 / (total_of(diagonal_in) + width * damping_in)
    scale_out = 1.0 / (total_of(diagonal_out) + width * damping_out)

    full_in_ref[...] = damped_in_ref[...]
    put_diagonal(diagonal_in, damping_in, full_in_ref)
    unpack_block(
        lambda position: got_out_ref[
            position % RING * CORES + position // RING, :rows_out, :
        ],
        damped_out_ref,
    )
    put_diagonal(diagonal_out, damping_out, damped_out_ref)

    chains = (
        (full_in_ref, iterate_in_ref, scale_in),
        (damped_out_ref, iterate_out_ref, scale_out),
    )
    rows, cols = tile_masks()
    for damped, iterate, scale in chains:
        factor = scale.astype(jnp.bfloat16).astype(jnp.float32)
        twice = jnp.where(rows == cols, 2.0 * scale, 0.0)
        for i in range(count):
            for j in range(count):
                place = (slice(i * TILE, (i + 1) * TILE), slice(j * TILE, (j + 1) * TILE))
                product = (damped[place].astype(jnp.float32) * factor).astype(jnp.bfloat16)
                moved = product.astype(jnp.float32) * factor
                iterate[place] = (twice - moved) if i == j else -moved

    for _ in range(ITERS - 1):
        currents = [iterate[...].astype(jnp.bfloat16) for _, iterate, _ in chains]
        products = [
            jnp.dot(damped[...], current, preferred_element_type=jnp.float32).astype(jnp.bfloat16)
            for (damped, _, _), current in zip(chains, currents)
        ]
        for (_, iterate, _), product, current in zip(chains, products, currents):
            iterate[...] = 2.0 * iterate[...] - jnp.dot(
                product, current, preferred_element_type=jnp.float32
            )
    inverse_ref[...] = iterate_in_ref[...].astype(jnp.bfloat16)
    right_ref[...] = iterate_out_ref[:, own_column].astype(jnp.bfloat16)


def finish_kernel(inverse_ref, right_ref, weight_ref, other_weight_ref, result_ref, left_ref):
    half = weight_ref.shape[1]
    parity = lax.axis_index("grp") % 2
    for ref, place in ((weight_ref, parity), (other_weight_ref, 1 - parity)):
        left_ref[:, pl.ds(pl.multiple_of(place * half, half), half)] = jnp.dot(
            inverse_ref[...], ref[...], preferred_element_type=jnp.float32
        ).astype(jnp.bfloat16)
    result_ref[...] = jnp.dot(
        left_ref[...], right_ref[...], preferred_element_type=jnp.float32
    ).astype(jnp.bfloat16)


VMEM_SPEC = pl.BlockSpec(memory_space=pltpu.VMEM)


def local_call(kernel, name, operands, outs, scratch=(), flops=0, space=pltpu.VMEM, limit=VMEM_LIMIT):
    multiple = isinstance(outs, tuple)
    listed = outs if multiple else (outs,)
    moved = sum(a.size * a.dtype.itemsize for a in operands + tuple(listed))
    return pl.pallas_call(
        kernel,
        out_shape=outs,
        in_specs=[pl.BlockSpec(memory_space=space)] * len(operands),
        out_specs=tuple([VMEM_SPEC] * len(listed)) if multiple else VMEM_SPEC,
        scratch_shapes=list(scratch),
        compiler_params=pltpu.CompilerParams(vmem_limit_bytes=limit),
        cost_estimate=pl.CostEstimate(flops=flops, bytes_accessed=moved, transcendentals=0),
        name=name,
    )(*operands)


def shape_of(*dims, dtype=jnp.float32):
    return jax.ShapeDtypeStruct(dims, dtype)


def exchange(value, axis, groups=None):
    return lax.all_to_all(value, axis, 0, 0, tiled=True, axis_index_groups=groups)


def swap_core(value):
    pairs = [(place, place ^ 1) for place in range(lax.axis_size("blk"))]
    return lax.ppermute(value, "blk", pairs)


def swap_along(value, stride, step):
    pairs = [(place, place ^ (stride * step)) for place in range(lax.axis_size("blk"))]
    return lax.ppermute(value, "blk", pairs)


def swap_half(value):
    pairs = [(place, place ^ 1) for place in range(lax.axis_size("grp"))]
    return lax.ppermute(value, "grp", pairs)


def shards(activations, output_grads, grad_weight):
    groups = lax.axis_size("grp")
    width = grad_weight.shape[0]
    half = grad_weight.shape[1]
    count = width // TILE
    packed_rows = width * width // (2 * TILE)
    total_tokens = activations.shape[0] * groups
    in_rows = packed_rows // groups
    share_rows = packed_rows // CORES
    piece_rows = share_rows // RING
    y_stride, x_stride = CORES, CORES * RING
    half_type = jnp.bfloat16

    other_grads = swap_half(output_grads)
    send_in = local_call(
        functools.partial(gram_in_kernel, total_tokens),
        "gram_in",
        (activations, output_grads),
        shape_of(groups, in_rows + EXTRA, TILE),
        scratch=[
            pltpu.VMEM(activations.shape, half_type),
            pltpu.VMEM(output_grads.shape, half_type),
            pltpu.SemaphoreType.DMA((CHUNKS + 1,)),
        ],
        flops=2 * activations.shape[0] * width * width,
        space=pltpu.HBM,
        limit=GRAM_LIMIT,
    )
    got_in = exchange(send_in, "grp")

    keep, give = local_call(
        functools.partial(gram_out_kernel, total_tokens),
        "gram_out",
        (output_grads, other_grads),
        (shape_of(share_rows + EXTRA, TILE),) * 2,
        scratch=[
            pltpu.VMEM((output_grads.shape[0], width), half_type),
            pltpu.VMEM((packed_rows, TILE), jnp.float32),
        ],
        flops=LATE_START * 3,
    )
    folds = (
        ("fold_cores", 1, share_rows // 2, swap_core),
        ("fold_x", 0, piece_rows, lambda value: swap_along(value, x_stride, 3)),
    )
    for name, bit, rows, swap in folds:
        keep, give = local_call(
            functools.partial(fold_kernel, bit),
            name,
            (keep, swap(give)),
            (shape_of(rows + EXTRA, TILE),) * 2,
        )
    to_all_in, extra_in, part_y = local_call(
        functools.partial(sum_both_kernel, count),
        "sum_both",
        (got_in, keep, swap_along(give, x_stride, 1)),
        (
            shape_of(groups, in_rows, TILE, dtype=half_type),
            shape_of(EXTRA, TILE),
            shape_of(piece_rows + EXTRA, TILE),
        ),
    )
    all_in = exchange(to_all_in, "grp")
    part_y = local_call(
        add_kernel,
        "add_y",
        (part_y, swap_along(part_y, y_stride, 1)),
        shape_of(*part_y.shape),
        flops=LATE_START,
    )
    to_all_out, extra_out = local_call(
        functools.partial(sum_y_kernel, count),
        "sum_y",
        (part_y, swap_along(part_y, y_stride, 3)),
        (
            shape_of(RING * CORES, piece_rows + EXTRA_HALF, TILE, dtype=half_type),
            shape_of(EXTRA, TILE),
        ),
    )
    same_y = [
        [x * x_stride + y * y_stride + core for x in range(RING) for core in range(CORES)]
        for y in range(RING)
    ]
    all_out = exchange(to_all_out, "blk", same_y)

    block = (width, width)
    all_in, extra_out = lax.optimization_barrier((all_in, extra_out))
    damped_in, sent_weight = local_call(
        unpack_in_kernel,
        "unpack_in",
        (all_in, grad_weight),
        (shape_of(*block, dtype=half_type), shape_of(*grad_weight.shape, dtype=half_type)),
    )
    other_weight = swap_half(sent_weight)
    extra_in = local_call(
        stage_kernel, "stage_extra", (damped_in, extra_in), shape_of(*extra_in.shape), flops=LATE_START
    )
    inverse_in, right = local_call(
        invert_kernel,
        "invert",
        (damped_in, all_out, extra_in, extra_out),
        (shape_of(*block, dtype=half_type), shape_of(width, half, dtype=half_type)),
        scratch=[
            pltpu.VMEM(block, half_type),
            pltpu.VMEM(block, half_type),
            pltpu.VMEM(block, jnp.float32),
            pltpu.VMEM(block, jnp.float32),
        ],
        flops=8 * (ITERS - 1) * width * width * width,
    )
    return local_call(
        finish_kernel,
        "finish",
        (inverse_in, right, grad_weight, other_weight),
        shape_of(width, half, dtype=half_type),
        scratch=[pltpu.VMEM(block, half_type)],
        flops=3 * width * width * width,
    )


def solution(mesh):
    in_specs = (P("grp", "blk"), P("blk", "grp"), P("blk", "grp"))
    out_specs = P("blk", "grp")
    return jax.shard_map(shards, mesh=mesh, in_specs=in_specs, out_specs=out_specs, check_vma=False)
```

```python
import functools

import jax
import jax.numpy as jnp
from jax import lax
from jax.experimental import pallas as pl
from jax.experimental.pallas import tpu as pltpu
from jax.sharding import PartitionSpec as P

ITERS = 6
DAMP_ROOT = 0.1
TILE = 128
CORES = 2
CHUNKS = 2
RING = 4
EXTRA = 8
EXTRA_HALF = 16
LATE_START = 10**10
VMEM_LIMIT = 48 * 1024 * 1024
GRAM_LIMIT = 58 * 1024 * 1024


def tile_plan(count):
    off = [(i, j) for i in range(count) for j in range(i + 1, count)]
    pairs = [(i, i + 1) for i in range(0, count, 2)]
    return off, pairs


def tile_masks():
    rows = lax.broadcasted_iota(jnp.int32, (TILE, TILE), 0)
    cols = lax.broadcasted_iota(jnp.int32, (TILE, TILE), 1)
    return rows, cols


def gram_parts(data):
    half = data.shape[1] // 2
    low, high = data[:, :half], data[:, half:]
    return [
        lax.dot_general(left, right, (((0,), (0,)), ((), ())), preferred_element_type=jnp.float32)
        for left, right in ((low, low), (low, high), (high, high))
    ]


def pack_gram(quarters, store):
    per = quarters[0].shape[0] // TILE
    count = 2 * per

    def tile(i, j):
        part = quarters[i // per + j // per]
        r, c = (i % per) * TILE, (j % per) * TILE
        return part[r : r + TILE, c : c + TILE]

    off, pairs = tile_plan(count)
    rows, cols = tile_masks()
    for position, (i, j) in enumerate(off):
        store(position, tile(i, j))
    for position, (i, j) in enumerate(pairs):
        store(len(off) + position, jnp.where(cols > rows, tile(i, i), tile(j, j)))
    return jnp.concatenate(
        [
            jnp.sum(jnp.where(rows == cols, tile(i, i), 0.0), axis=0, keepdims=True)
            for i in range(count)
        ],
        axis=0,
    )


def unpack_block(fetch, out_ref):
    count = out_ref.shape[0] // TILE
    off, pairs = tile_plan(count)
    rows, cols = tile_masks()

    def put(i, j, value):
        out_ref[i * TILE : (i + 1) * TILE, j * TILE : (j + 1) * TILE] = value.astype(jnp.bfloat16)

    for position, (i, j) in enumerate(off):
        value = fetch(position).astype(jnp.float32)
        put(i, j, value)
        put(j, i, value.T)
    for position, (i, j) in enumerate(pairs):
        value = fetch(len(off) + position).astype(jnp.float32)
        other = value.T
        put(i, i, jnp.where(cols > rows, value, other))
        put(j, j, jnp.where(cols < rows, value, other))


def put_diagonal(diagonal, damping, out_ref):
    rows, cols = tile_masks()
    for i in range(out_ref.shape[0] // TILE):
        place = (slice(i * TILE, (i + 1) * TILE),) * 2
        damped = diagonal[i : i + 1, :] + damping
        tile = out_ref[place].astype(jnp.float32)
        out_ref[place] = jnp.where(rows == cols, damped, tile).astype(jnp.bfloat16)


def total_of(value):
    return jnp.sum(jnp.sum(value, axis=1, keepdims=True), axis=0, keepdims=True)


def gram_in_kernel(tokens, data_hbm, grads_hbm, out_ref, data_ref, grads_ref, sems):
    pieces, piece_rows = out_ref.shape[0], out_ref.shape[1] - EXTRA
    per_tile = TILE // piece_rows
    scale = 1.0 / tokens
    rows = data_ref.shape[0] // CHUNKS
    copies = []
    for chunk in range(CHUNKS):
        place = pl.ds(chunk * rows, rows)
        copies.append(
            pltpu.make_async_copy(data_hbm.at[place], data_ref.at[place], sems.at[chunk])
        )
    copies.append(pltpu.make_async_copy(grads_hbm, grads_ref, sems.at[CHUNKS]))
    for copy in copies[CHUNKS:] + copies[:CHUNKS]:
        copy.start()
    copies[CHUNKS].wait()
    grads = grads_ref[...].astype(jnp.float32)
    energy = total_of(grads * grads) * scale
    for chunk in range(CHUNKS):
        copies[chunk].wait()
        part = gram_parts(data_ref[chunk * rows : (chunk + 1) * rows, :])
        quarters = part if chunk == 0 else [old + new for old, new in zip(quarters, part)]

    def store(position, value):
        for part in range(per_tile):
            out_ref[position * per_tile + part, :piece_rows, :] = value[
                part * piece_rows : (part + 1) * piece_rows
            ]

    diagonal = pack_gram([scale * quarter for quarter in quarters], store)
    filler = jnp.zeros((EXTRA - diagonal.shape[0] - 1, TILE), jnp.float32)
    extra = jnp.concatenate(
        [diagonal, jnp.broadcast_to(energy, (1, TILE)), filler], axis=0
    )
    for piece in range(pieces):
        out_ref[piece, piece_rows:, :] = extra


def gram_out_kernel(tokens, own_ref, other_ref, keep_ref, send_ref, data_ref, packed_ref):
    half = own_ref.shape[1]
    parity = lax.axis_index("grp") % 2
    core = lax.axis_index("blk") % CORES
    data_ref[:, pl.ds(pl.multiple_of(parity * half, half), half)] = own_ref[...]
    data_ref[:, pl.ds(pl.multiple_of((1 - parity) * half, half), half)] = other_ref[...]

    def store(position, value):
        packed_ref[position * TILE : (position + 1) * TILE, :] = value

    scale = 1.0 / tokens
    diagonal = pack_gram([scale * part for part in gram_parts(data_ref[...])], store)
    filler = jnp.zeros((EXTRA - diagonal.shape[0], TILE), jnp.float32)
    extra = jnp.concatenate([diagonal, filler], axis=0)
    share = keep_ref.shape[0] - EXTRA
    for ref, owner in ((keep_ref, core), (send_ref, 1 - core)):
        start = pl.multiple_of(owner * share, share)
        ref[:share, :] = packed_ref[pl.ds(start, share), :]
        ref[share:, :] = extra


def along_x():
    return lax.axis_index("blk") // (RING * CORES)


def fold_kernel(bit, left_ref, right_ref, keep_ref, give_ref):
    rows = keep_ref.shape[0] - EXTRA
    extra = left_ref[2 * rows :, :] + right_ref[2 * rows :, :]
    own = (along_x() >> bit) & 1
    for ref, owner in ((keep_ref, own), (give_ref, 1 - own)):
        place = pl.ds(pl.multiple_of(owner * rows, rows), rows)
        ref[:rows, :] = left_ref[place, :] + right_ref[place, :]
        ref[rows:, :] = extra


def stage_kernel(after_ref, value_ref, out_ref):
    out_ref[...] = value_ref[...]


def add_kernel(left_ref, right_ref, out_ref):
    out_ref[...] = left_ref[...] + right_ref[...]


def sum_pieces(ref):
    total = ref[0]
    for piece in range(1, ref.shape[0]):
        total = total + ref[piece]
    return total


def split_rows(value):
    high = value.astype(jnp.bfloat16).astype(jnp.float32)
    rest = value - high
    middle = rest.astype(jnp.bfloat16).astype(jnp.float32)
    return [high, middle, rest - middle]


def sum_in_kernel(got_ref, after_ref, send_ref, extra_ref):
    total = sum_pieces(got_ref)
    rows = send_ref.shape[1]
    rounded = total[:rows].astype(jnp.bfloat16)
    for piece in range(send_ref.shape[0]):
        send_ref[piece] = rounded
    extra_ref[...] = total[rows:]


def sum_x_kernel(count, left_ref, right_ref, extra_in_ref, out_ref):
    extra = extra_in_ref[...]
    total = left_ref[...] + right_ref[...]
    rows = total.shape[0] - EXTRA
    trace_in = jnp.broadcast_to(total_of(extra[:count]), (1, TILE))
    energy_out = extra[count : count + 1]
    filler = jnp.zeros((EXTRA - count - 2, TILE), jnp.float32)
    out_ref[...] = jnp.concatenate(
        [total[: rows + count], trace_in, energy_out, filler], axis=0
    )


def sum_y_kernel(count, left_ref, right_ref, send_ref, extra_ref):
    total = left_ref[...] + right_ref[...]
    rows = total.shape[0] - EXTRA
    extra = total[rows:]
    scalars = split_rows(extra[count : count + 1]) + split_rows(extra[count + 1 : count + 2])
    filler = jnp.zeros((EXTRA_HALF - len(scalars), TILE), jnp.float32)
    block = jnp.concatenate([total[:rows]] + scalars + [filler], axis=0).astype(jnp.bfloat16)
    for piece in range(send_ref.shape[0]):
        send_ref[piece] = block
    extra_ref[...] = extra


def stage_in_kernel(got_ref, weight_ref, sent_ref, sent_weight_ref):
    sent_ref[...] = got_ref[...]
    sent_weight_ref[...] = weight_ref[...]


def unpack_in_kernel(got_ref, other_ref, out_ref, packed_ref):
    rows = got_ref.shape[1]
    parity = lax.axis_index("grp") % 2
    for ref, place in ((got_ref, parity), (other_ref, 1 - parity)):
        for piece in range(ref.shape[0]):
            start = pl.multiple_of((2 * piece + place) * rows, rows)
            packed_ref[pl.ds(start, rows), :] = ref[piece]
    unpack_block(lambda position: packed_ref[position * TILE : (position + 1) * TILE, :], out_ref)


def invert_kernel(
    damped_in_ref,
    got_out_ref,
    extra_in_ref,
    extra_out_ref,
    inverse_ref,
    right_ref,
    full_in_ref,
    damped_out_ref,
    iterate_in_ref,
    iterate_out_ref,
):
    width = damped_in_ref.shape[0]
    count = width // TILE
    half = right_ref.shape[1]
    parity = lax.axis_index("grp") % 2
    pieces, rows_out = got_out_ref.shape[0], got_out_ref.shape[1] - EXTRA_HALF
    own_column = pl.ds(pl.multiple_of(parity * half, half), half)

    scalars = jnp.zeros((EXTRA_HALF, TILE), jnp.float32)
    for piece in range(pieces):
        scalars = scalars + got_out_ref[piece, rows_out:, :].astype(jnp.float32)
    sum_in = scalars[0:1] + scalars[1:2] + scalars[2:3]
    sum_out = scalars[3:4] + scalars[4:5] + scalars[5:6]
    owners = lax.axis_size("blk")
    blocks_out = lax.axis_size("grp") // 2
    pi_ratio = jnp.sqrt((sum_in / (owners * width)) / (sum_out / (blocks_out * width)))
    damping_in = DAMP_ROOT * pi_ratio
    damping_out = DAMP_ROOT / pi_ratio
    diagonal_in = extra_in_ref[:count, :]
    diagonal_out = extra_out_ref[:count, :]
    scale_in = 1.0 / (total_of(diagonal_in) + width * damping_in)
    scale_out = 1.0 / (total_of(diagonal_out) + width * damping_out)

    full_in_ref[...] = damped_in_ref[...]
    put_diagonal(diagonal_in, damping_in, full_in_ref)
    unpack_block(
        lambda position: got_out_ref[
            position % RING * CORES + position // RING, :rows_out, :
        ],
        damped_out_ref,
    )
    put_diagonal(diagonal_out, damping_out, damped_out_ref)

    chains = (
        (full_in_ref, iterate_in_ref, scale_in),
        (damped_out_ref, iterate_out_ref, scale_out),
    )
    rows, cols = tile_masks()
    for damped, iterate, scale in chains:
        factor = scale.astype(jnp.bfloat16).astype(jnp.float32)
        twice = jnp.where(rows == cols, 2.0 * scale, 0.0)
        for i in range(count):
            for j in range(count):
                place = (slice(i * TILE, (i + 1) * TILE), slice(j * TILE, (j + 1) * TILE))
                product = (damped[place].astype(jnp.float32) * factor).astype(jnp.bfloat16)
                moved = product.astype(jnp.float32) * factor
                iterate[place] = (twice - moved) if i == j else -moved

    for _ in range(ITERS - 1):
        currents = [iterate[...].astype(jnp.bfloat16) for _, iterate, _ in chains]
        products = [
            jnp.dot(damped[...], current, preferred_element_type=jnp.float32).astype(jnp.bfloat16)
            for (damped, _, _), current in zip(chains, currents)
        ]
        for (_, iterate, _), product, current in zip(chains, products, currents):
            iterate[...] = 2.0 * iterate[...] - jnp.dot(
                product, current, preferred_element_type=jnp.float32
            )
    inverse_ref[...] = iterate_in_ref[...].astype(jnp.bfloat16)
    right_ref[...] = iterate_out_ref[:, own_column].astype(jnp.bfloat16)


def finish_kernel(inverse_ref, right_ref, weight_ref, other_weight_ref, result_ref, left_ref):
    half = weight_ref.shape[1]
    parity = lax.axis_index("grp") % 2
    for ref, place in ((weight_ref, parity), (other_weight_ref, 1 - parity)):
        left_ref[:, pl.ds(pl.multiple_of(place * half, half), half)] = jnp.dot(
            inverse_ref[...], ref[...], preferred_element_type=jnp.float32
        ).astype(jnp.bfloat16)
    result_ref[...] = jnp.dot(
        left_ref[...], right_ref[...], preferred_element_type=jnp.float32
    ).astype(jnp.bfloat16)


VMEM_SPEC = pl.BlockSpec(memory_space=pltpu.VMEM)


def local_call(kernel, name, operands, outs, scratch=(), flops=0, space=pltpu.VMEM, limit=VMEM_LIMIT):
    multiple = isinstance(outs, tuple)
    listed = outs if multiple else (outs,)
    moved = sum(a.size * a.dtype.itemsize for a in operands + tuple(listed))
    return pl.pallas_call(
        kernel,
        out_shape=outs,
        in_specs=[pl.BlockSpec(memory_space=space)] * len(operands),
        out_specs=tuple([VMEM_SPEC] * len(listed)) if multiple else VMEM_SPEC,
        scratch_shapes=list(scratch),
        compiler_params=pltpu.CompilerParams(vmem_limit_bytes=limit),
        cost_estimate=pl.CostEstimate(flops=flops, bytes_accessed=moved, transcendentals=0),
        name=name,
    )(*operands)


def shape_of(*dims, dtype=jnp.float32):
    return jax.ShapeDtypeStruct(dims, dtype)


def exchange(value, axis, groups=None):
    return lax.all_to_all(value, axis, 0, 0, tiled=True, axis_index_groups=groups)


def swap_core(value):
    pairs = [(place, place ^ 1) for place in range(lax.axis_size("blk"))]
    return lax.ppermute(value, "blk", pairs)


def swap_along(value, stride, step):
    pairs = [(place, place ^ (stride * step)) for place in range(lax.axis_size("blk"))]
    return lax.ppermute(value, "blk", pairs)


def swap_half(value):
    pairs = [(place, place ^ 1) for place in range(lax.axis_size("grp"))]
    return lax.ppermute(value, "grp", pairs)


def shards(activations, output_grads, grad_weight):
    groups = lax.axis_size("grp")
    width = grad_weight.shape[0]
    half = grad_weight.shape[1]
    count = width // TILE
    packed_rows = width * width // (2 * TILE)
    total_tokens = activations.shape[0] * groups
    in_rows = packed_rows // groups
    share_rows = packed_rows // CORES
    piece_rows = share_rows // RING
    y_stride, x_stride = CORES, CORES * RING
    half_type = jnp.bfloat16

    other_grads = swap_half(output_grads)
    send_in = local_call(
        functools.partial(gram_in_kernel, total_tokens),
        "gram_in",
        (activations, output_grads),
        shape_of(groups, in_rows + EXTRA, TILE),
        scratch=[
            pltpu.VMEM(activations.shape, half_type),
            pltpu.VMEM(output_grads.shape, half_type),
            pltpu.SemaphoreType.DMA((CHUNKS + 1,)),
        ],
        flops=2 * activations.shape[0] * width * width,
        space=pltpu.HBM,
        limit=GRAM_LIMIT,
    )
    got_in = exchange(send_in, "grp")

    keep, give = local_call(
        functools.partial(gram_out_kernel, total_tokens),
        "gram_out",
        (output_grads, other_grads),
        (shape_of(share_rows + EXTRA, TILE),) * 2,
        scratch=[
            pltpu.VMEM((output_grads.shape[0], width), half_type),
            pltpu.VMEM((packed_rows, TILE), jnp.float32),
        ],
        flops=LATE_START * 3,
    )
    folds = (
        ("fold_cores", 1, share_rows // 2, swap_core),
        ("fold_x", 0, piece_rows, lambda value: swap_along(value, x_stride, 3)),
    )
    for name, bit, rows, swap in folds:
        keep, give = local_call(
            functools.partial(fold_kernel, bit),
            name,
            (keep, swap(give)),
            (shape_of(rows + EXTRA, TILE),) * 2,
        )
    to_all_in, extra_in = local_call(
        sum_in_kernel,
        "sum_in",
        (got_in, keep),
        (shape_of(groups // 2, in_rows, TILE, dtype=half_type), shape_of(EXTRA, TILE)),
    )
    same_half = [list(range(parity, groups, 2)) for parity in range(2)]
    all_in = exchange(to_all_in, "grp", same_half)
    part_y = local_call(
        functools.partial(sum_x_kernel, count),
        "sum_x",
        (keep, swap_along(give, x_stride, 1), extra_in),
        shape_of(piece_rows + EXTRA, TILE),
        flops=LATE_START,
    )
    part_y = local_call(
        add_kernel,
        "add_y",
        (part_y, swap_along(part_y, y_stride, 1)),
        shape_of(*part_y.shape),
        flops=LATE_START,
    )
    to_all_out, extra_out = local_call(
        functools.partial(sum_y_kernel, count),
        "sum_y",
        (part_y, swap_along(part_y, y_stride, 3)),
        (
            shape_of(RING * CORES, piece_rows + EXTRA_HALF, TILE, dtype=half_type),
            shape_of(EXTRA, TILE),
        ),
    )
    same_y = [
        [x * x_stride + y * y_stride + core for x in range(RING) for core in range(CORES)]
        for y in range(RING)
    ]
    all_out = exchange(to_all_out, "blk", same_y)

    block = (width, width)
    all_in, extra_out = lax.optimization_barrier((all_in, extra_out))
    sent_in, sent_weight = local_call(
        stage_in_kernel,
        "stage_in",
        (all_in, grad_weight),
        (
            shape_of(*all_in.shape, dtype=half_type),
            shape_of(*grad_weight.shape, dtype=half_type),
        ),
    )
    other_in = swap_half(sent_in)
    other_weight = swap_half(sent_weight)
    extra_in = local_call(
        stage_kernel, "stage_extra", (sent_in, extra_in), shape_of(*extra_in.shape), flops=LATE_START
    )
    damped_in = local_call(
        unpack_in_kernel,
        "unpack_in",
        (all_in, other_in),
        shape_of(*block, dtype=half_type),
        scratch=[pltpu.VMEM((packed_rows, TILE), half_type)],
    )
    inverse_in, right = local_call(
        invert_kernel,
        "invert",
        (damped_in, all_out, extra_in, extra_out),
        (shape_of(*block, dtype=half_type), shape_of(width, half, dtype=half_type)),
        scratch=[
            pltpu.VMEM(block, half_type),
            pltpu.VMEM(block, half_type),
            pltpu.VMEM(block, jnp.float32),
            pltpu.VMEM(block, jnp.float32),
        ],
        flops=8 * (ITERS - 1) * width * width * width,
    )
    return local_call(
        finish_kernel,
        "finish",
        (inverse_in, right, grad_weight, other_weight),
        shape_of(width, half, dtype=half_type),
        scratch=[pltpu.VMEM(block, half_type)],
        flops=3 * width * width * width,
    )


def solution(mesh):
    in_specs = (P("grp", "blk"), P("blk", "grp"), P("blk", "grp"))
    out_specs = P("blk", "grp")
    return jax.shard_map(shards, mesh=mesh, in_specs=in_specs, out_specs=out_specs, check_vma=False)
```

```python
import functools

import jax
import jax.numpy as jnp
from jax import lax
from jax.experimental import pallas as pl
from jax.experimental.pallas import tpu as pltpu
from jax.sharding import PartitionSpec as P

ITERS = 6
DAMP_ROOT = 0.1
TILE = 128
CORES = 2
CHUNKS = 2
RING = 4
EXTRA = 8
EXTRA_HALF = 16
LATE_START = 10**10
VMEM_LIMIT = 48 * 1024 * 1024
GRAM_LIMIT = 58 * 1024 * 1024


def tile_plan(count):
    off = [(i, j) for i in range(count) for j in range(i + 1, count)]
    pairs = [(i, i + 1) for i in range(0, count, 2)]
    return off, pairs


def tile_masks():
    rows = lax.broadcasted_iota(jnp.int32, (TILE, TILE), 0)
    cols = lax.broadcasted_iota(jnp.int32, (TILE, TILE), 1)
    return rows, cols


def gram_parts(data):
    half = data.shape[1] // 2
    low, high = data[:, :half], data[:, half:]
    return [
        lax.dot_general(left, right, (((0,), (0,)), ((), ())), preferred_element_type=jnp.float32)
        for left, right in ((low, low), (low, high), (high, high))
    ]


def pack_gram(quarters, store):
    per = quarters[0].shape[0] // TILE
    count = 2 * per

    def tile(i, j):
        part = quarters[i // per + j // per]
        r, c = (i % per) * TILE, (j % per) * TILE
        return part[r : r + TILE, c : c + TILE]

    off, pairs = tile_plan(count)
    rows, cols = tile_masks()
    for position, (i, j) in enumerate(off):
        store(position, tile(i, j))
    for position, (i, j) in enumerate(pairs):
        store(len(off) + position, jnp.where(cols > rows, tile(i, i), tile(j, j)))
    return jnp.concatenate(
        [
            jnp.sum(jnp.where(rows == cols, tile(i, i), 0.0), axis=0, keepdims=True)
            for i in range(count)
        ],
        axis=0,
    )


def unpack_block(fetch, out_ref):
    count = out_ref.shape[0] // TILE
    off, pairs = tile_plan(count)
    rows, cols = tile_masks()

    def put(i, j, value):
        out_ref[i * TILE : (i + 1) * TILE, j * TILE : (j + 1) * TILE] = value.astype(jnp.bfloat16)

    for position, (i, j) in enumerate(off):
        value = fetch(position).astype(jnp.float32)
        put(i, j, value)
        put(j, i, value.T)
    for position, (i, j) in enumerate(pairs):
        value = fetch(len(off) + position).astype(jnp.float32)
        other = value.T
        put(i, i, jnp.where(cols > rows, value, other))
        put(j, j, jnp.where(cols < rows, value, other))


def put_diagonal(diagonal, damping, out_ref):
    rows, cols = tile_masks()
    for i in range(out_ref.shape[0] // TILE):
        place = (slice(i * TILE, (i + 1) * TILE),) * 2
        damped = diagonal[i : i + 1, :] + damping
        tile = out_ref[place].astype(jnp.float32)
        out_ref[place] = jnp.where(rows == cols, damped, tile).astype(jnp.bfloat16)


def total_of(value):
    return jnp.sum(jnp.sum(value, axis=1, keepdims=True), axis=0, keepdims=True)


def gram_in_kernel(tokens, data_hbm, grads_hbm, out_ref, data_ref, grads_ref, sems):
    pieces, piece_rows = out_ref.shape[0], out_ref.shape[1] - EXTRA
    per_tile = TILE // piece_rows
    scale = 1.0 / tokens
    rows = data_ref.shape[0] // CHUNKS
    copies = []
    for chunk in range(CHUNKS):
        place = pl.ds(chunk * rows, rows)
        copies.append(
            pltpu.make_async_copy(data_hbm.at[place], data_ref.at[place], sems.at[chunk])
        )
    copies.append(pltpu.make_async_copy(grads_hbm, grads_ref, sems.at[CHUNKS]))
    for copy in copies[CHUNKS:] + copies[:CHUNKS]:
        copy.start()
    copies[CHUNKS].wait()
    grads = grads_ref[...].astype(jnp.float32)
    energy = total_of(grads * grads) * scale
    for chunk in range(CHUNKS):
        copies[chunk].wait()
        part = gram_parts(data_ref[chunk * rows : (chunk + 1) * rows, :])
        quarters = part if chunk == 0 else [old + new for old, new in zip(quarters, part)]

    def store(position, value):
        for part in range(per_tile):
            out_ref[position * per_tile + part, :piece_rows, :] = value[
                part * piece_rows : (part + 1) * piece_rows
            ]

    diagonal = pack_gram([scale * quarter for quarter in quarters], store)
    filler = jnp.zeros((EXTRA - diagonal.shape[0] - 1, TILE), jnp.float32)
    extra = jnp.concatenate(
        [diagonal, jnp.broadcast_to(energy, (1, TILE)), filler], axis=0
    )
    for piece in range(pieces):
        out_ref[piece, piece_rows:, :] = extra


def gram_out_kernel(tokens, own_ref, other_ref, keep_ref, send_ref, data_ref, packed_ref):
    half = own_ref.shape[1]
    parity = lax.axis_index("grp") % 2
    core = lax.axis_index("blk") % CORES
    data_ref[:, pl.ds(pl.multiple_of(parity * half, half), half)] = own_ref[...]
    data_ref[:, pl.ds(pl.multiple_of((1 - parity) * half, half), half)] = other_ref[...]

    def store(position, value):
        packed_ref[position * TILE : (position + 1) * TILE, :] = value

    scale = 1.0 / tokens
    diagonal = pack_gram([scale * part for part in gram_parts(data_ref[...])], store)
    filler = jnp.zeros((EXTRA - diagonal.shape[0], TILE), jnp.float32)
    extra = jnp.concatenate([diagonal, filler], axis=0)
    share = keep_ref.shape[0] - EXTRA
    for ref, owner in ((keep_ref, core), (send_ref, 1 - core)):
        start = pl.multiple_of((parity * CORES + owner) * share, share)
        ref[:share, :] = packed_ref[pl.ds(start, share), :]
        ref[share:, :] = extra


def along_x():
    return lax.axis_index("blk") // (RING * CORES)


def fold_kernel(bit, left_ref, right_ref, keep_ref, give_ref):
    rows = keep_ref.shape[0] - EXTRA
    extra = left_ref[2 * rows :, :] + right_ref[2 * rows :, :]
    own = (along_x() >> bit) & 1
    for ref, owner in ((keep_ref, own), (give_ref, 1 - own)):
        place = pl.ds(pl.multiple_of(owner * rows, rows), rows)
        ref[:rows, :] = left_ref[place, :] + right_ref[place, :]
        ref[rows:, :] = extra


def stage_kernel(after_ref, value_ref, out_ref):
    out_ref[...] = value_ref[...]


def add_kernel(left_ref, right_ref, out_ref):
    out_ref[...] = left_ref[...] + right_ref[...]


def sum_pieces(ref):
    total = ref[0]
    for piece in range(1, ref.shape[0]):
        total = total + ref[piece]
    return total


def split_rows(value):
    high = value.astype(jnp.bfloat16).astype(jnp.float32)
    rest = value - high
    middle = rest.astype(jnp.bfloat16).astype(jnp.float32)
    return [high, middle, rest - middle]


def sum_in_kernel(got_ref, after_ref, send_ref, extra_ref):
    total = sum_pieces(got_ref)
    rows = send_ref.shape[1]
    rounded = total[:rows].astype(jnp.bfloat16)
    for piece in range(send_ref.shape[0]):
        send_ref[piece] = rounded
    extra_ref[...] = total[rows:]


def sum_x_kernel(count, left_ref, right_ref, extra_in_ref, out_ref):
    extra = extra_in_ref[...]
    total = left_ref[...] + right_ref[...]
    rows = total.shape[0] - EXTRA
    trace_in = jnp.broadcast_to(total_of(extra[:count]), (1, TILE))
    energy_out = extra[count : count + 1]
    filler = jnp.zeros((EXTRA - count - 2, TILE), jnp.float32)
    out_ref[...] = jnp.concatenate(
        [total[: rows + count], trace_in, energy_out, filler], axis=0
    )


def sum_y_kernel(count, left_ref, right_ref, send_ref, extra_ref):
    total = left_ref[...] + right_ref[...]
    rows = total.shape[0] - EXTRA
    extra = total[rows:]
    scalars = split_rows(extra[count : count + 1]) + split_rows(extra[count + 1 : count + 2])
    filler = jnp.zeros((EXTRA_HALF - len(scalars), TILE), jnp.float32)
    block = jnp.concatenate([total[:rows]] + scalars + [filler], axis=0).astype(jnp.bfloat16)
    for piece in range(send_ref.shape[0]):
        send_ref[piece] = block
    extra_ref[...] = extra


def stage_in_kernel(got_ref, weight_ref, sent_ref, sent_weight_ref):
    sent_ref[...] = got_ref[...]
    sent_weight_ref[...] = weight_ref[...]


def unpack_in_kernel(got_ref, other_ref, out_ref, packed_ref):
    rows = got_ref.shape[1]
    parity = lax.axis_index("grp") % 2
    for ref, place in ((got_ref, parity), (other_ref, 1 - parity)):
        for piece in range(ref.shape[0]):
            start = pl.multiple_of((2 * piece + place) * rows, rows)
            packed_ref[pl.ds(start, rows), :] = ref[piece]
    unpack_block(lambda position: packed_ref[position * TILE : (position + 1) * TILE, :], out_ref)


def invert_kernel(
    damped_in_ref,
    got_out_ref,
    extra_in_ref,
    extra_out_ref,
    inverse_ref,
    right_ref,
    full_in_ref,
    damped_out_ref,
    iterate_in_ref,
    iterate_out_ref,
):
    width = damped_in_ref.shape[0]
    count = width // TILE
    half = right_ref.shape[1]
    parity = lax.axis_index("grp") % 2
    pieces, rows_out = got_out_ref.shape[0], got_out_ref.shape[1] - EXTRA_HALF
    own_column = pl.ds(pl.multiple_of(parity * half, half), half)

    scalars = jnp.zeros((EXTRA_HALF, TILE), jnp.float32)
    for piece in range(pieces // 2):
        scalars = scalars + got_out_ref[piece, rows_out:, :].astype(jnp.float32)
    sum_in = scalars[0:1] + scalars[1:2] + scalars[2:3]
    sum_out = scalars[3:4] + scalars[4:5] + scalars[5:6]
    owners = lax.axis_size("blk")
    blocks_out = lax.axis_size("grp") // 2
    pi_ratio = jnp.sqrt((sum_in / (owners * width)) / (sum_out / (blocks_out * width)))
    damping_in = DAMP_ROOT * pi_ratio
    damping_out = DAMP_ROOT / pi_ratio
    diagonal_in = extra_in_ref[:count, :]
    diagonal_out = extra_out_ref[:count, :]
    scale_in = 1.0 / (total_of(diagonal_in) + width * damping_in)
    scale_out = 1.0 / (total_of(diagonal_out) + width * damping_out)

    full_in_ref[...] = damped_in_ref[...]
    put_diagonal(diagonal_in, damping_in, full_in_ref)
    def fetch_out(position):
        per_tile = TILE // rows_out
        pair = position // RING
        core, first = position % RING // CORES, position % CORES * per_tile
        return jnp.concatenate(
            [
                got_out_ref[(pair * RING + first + part) * CORES + core, :rows_out, :]
                for part in range(per_tile)
            ],
            axis=0,
        )

    unpack_block(fetch_out, damped_out_ref)
    put_diagonal(diagonal_out, damping_out, damped_out_ref)

    chains = (
        (full_in_ref, iterate_in_ref, scale_in),
        (damped_out_ref, iterate_out_ref, scale_out),
    )
    rows, cols = tile_masks()
    for damped, iterate, scale in chains:
        factor = scale.astype(jnp.bfloat16).astype(jnp.float32)
        twice = jnp.where(rows == cols, 2.0 * scale, 0.0)
        for i in range(count):
            for j in range(count):
                place = (slice(i * TILE, (i + 1) * TILE), slice(j * TILE, (j + 1) * TILE))
                product = (damped[place].astype(jnp.float32) * factor).astype(jnp.bfloat16)
                moved = product.astype(jnp.float32) * factor
                iterate[place] = (twice - moved) if i == j else -moved

    for _ in range(ITERS - 1):
        currents = [iterate[...].astype(jnp.bfloat16) for _, iterate, _ in chains]
        products = [
            jnp.dot(damped[...], current, preferred_element_type=jnp.float32).astype(jnp.bfloat16)
            for (damped, _, _), current in zip(chains, currents)
        ]
        for (_, iterate, _), product, current in zip(chains, products, currents):
            iterate[...] = 2.0 * iterate[...] - jnp.dot(
                product, current, preferred_element_type=jnp.float32
            )
    inverse_ref[...] = iterate_in_ref[...].astype(jnp.bfloat16)
    right_ref[...] = iterate_out_ref[:, own_column].astype(jnp.bfloat16)


def finish_kernel(inverse_ref, right_ref, weight_ref, other_weight_ref, result_ref, left_ref):
    half = weight_ref.shape[1]
    parity = lax.axis_index("grp") % 2
    for ref, place in ((weight_ref, parity), (other_weight_ref, 1 - parity)):
        left_ref[:, pl.ds(pl.multiple_of(place * half, half), half)] = jnp.dot(
            inverse_ref[...], ref[...], preferred_element_type=jnp.float32
        ).astype(jnp.bfloat16)
    result_ref[...] = jnp.dot(
        left_ref[...], right_ref[...], preferred_element_type=jnp.float32
    ).astype(jnp.bfloat16)


VMEM_SPEC = pl.BlockSpec(memory_space=pltpu.VMEM)


def local_call(kernel, name, operands, outs, scratch=(), flops=0, space=pltpu.VMEM, limit=VMEM_LIMIT):
    multiple = isinstance(outs, tuple)
    listed = outs if multiple else (outs,)
    moved = sum(a.size * a.dtype.itemsize for a in operands + tuple(listed))
    return pl.pallas_call(
        kernel,
        out_shape=outs,
        in_specs=[pl.BlockSpec(memory_space=space)] * len(operands),
        out_specs=tuple([VMEM_SPEC] * len(listed)) if multiple else VMEM_SPEC,
        scratch_shapes=list(scratch),
        compiler_params=pltpu.CompilerParams(vmem_limit_bytes=limit),
        cost_estimate=pl.CostEstimate(flops=flops, bytes_accessed=moved, transcendentals=0),
        name=name,
    )(*operands)


def shape_of(*dims, dtype=jnp.float32):
    return jax.ShapeDtypeStruct(dims, dtype)


def exchange(value, axis, groups=None):
    return lax.all_to_all(value, axis, 0, 0, tiled=True, axis_index_groups=groups)


def swap_core(value):
    pairs = [(place, place ^ 1) for place in range(lax.axis_size("blk"))]
    return lax.ppermute(value, "blk", pairs)


def swap_along(value, stride, step):
    pairs = [(place, place ^ (stride * step)) for place in range(lax.axis_size("blk"))]
    return lax.ppermute(value, "blk", pairs)


def swap_half(value):
    pairs = [(place, place ^ 1) for place in range(lax.axis_size("grp"))]
    return lax.ppermute(value, "grp", pairs)


def shards(activations, output_grads, grad_weight):
    groups = lax.axis_size("grp")
    width = grad_weight.shape[0]
    half = grad_weight.shape[1]
    count = width // TILE
    packed_rows = width * width // (2 * TILE)
    total_tokens = activations.shape[0] * groups
    in_rows = packed_rows // groups
    share_rows = packed_rows // (2 * CORES)
    piece_rows = share_rows // RING
    y_stride, x_stride = CORES, CORES * RING
    half_type = jnp.bfloat16

    other_grads = swap_half(output_grads)
    send_in = local_call(
        functools.partial(gram_in_kernel, total_tokens),
        "gram_in",
        (activations, output_grads),
        shape_of(groups, in_rows + EXTRA, TILE),
        scratch=[
            pltpu.VMEM(activations.shape, half_type),
            pltpu.VMEM(output_grads.shape, half_type),
            pltpu.SemaphoreType.DMA((CHUNKS + 1,)),
        ],
        flops=2 * activations.shape[0] * width * width,
        space=pltpu.HBM,
        limit=GRAM_LIMIT,
    )
    got_in = exchange(send_in, "grp")

    keep, give = local_call(
        functools.partial(gram_out_kernel, total_tokens),
        "gram_out",
        (output_grads, other_grads),
        (shape_of(share_rows + EXTRA, TILE),) * 2,
        scratch=[
            pltpu.VMEM((output_grads.shape[0], width), half_type),
            pltpu.VMEM((packed_rows, TILE), jnp.float32),
        ],
        flops=LATE_START * 3,
    )
    folds = (
        ("fold_cores", 1, share_rows // 2, swap_core),
        ("fold_x", 0, piece_rows, lambda value: swap_along(value, x_stride, 3)),
    )
    for name, bit, rows, swap in folds:
        keep, give = local_call(
            functools.partial(fold_kernel, bit),
            name,
            (keep, swap(give)),
            (shape_of(rows + EXTRA, TILE),) * 2,
        )
    to_all_in, extra_in = local_call(
        sum_in_kernel,
        "sum_in",
        (got_in, keep),
        (shape_of(groups // 2, in_rows, TILE, dtype=half_type), shape_of(EXTRA, TILE)),
    )
    same_half = [list(range(parity, groups, 2)) for parity in range(2)]
    all_in = exchange(to_all_in, "grp", same_half)
    part_y = local_call(
        functools.partial(sum_x_kernel, count),
        "sum_x",
        (keep, swap_along(give, x_stride, 1), extra_in),
        shape_of(piece_rows + EXTRA, TILE),
        flops=LATE_START,
    )
    part_y = local_call(
        add_kernel,
        "add_y",
        (part_y, swap_along(part_y, y_stride, 1)),
        shape_of(*part_y.shape),
        flops=LATE_START,
    )
    to_all_out, extra_out = local_call(
        functools.partial(sum_y_kernel, count),
        "sum_y",
        (part_y, swap_along(part_y, y_stride, 3)),
        (
            shape_of(2 * RING * CORES, piece_rows + EXTRA_HALF, TILE, dtype=half_type),
            shape_of(EXTRA, TILE),
        ),
    )
    owners = lax.axis_size("blk")
    same_plane = [
        [
            (2 * z + parity) * owners + x * x_stride + y * y_stride + core
            for parity in range(2)
            for x in range(RING)
            for core in range(CORES)
        ]
        for z in range(groups // 2)
        for y in range(RING)
    ]
    all_out = exchange(to_all_out, ("grp", "blk"), same_plane)

    block = (width, width)
    all_in, extra_out = lax.optimization_barrier((all_in, extra_out))
    sent_in, sent_weight = local_call(
        stage_in_kernel,
        "stage_in",
        (all_in, grad_weight),
        (
            shape_of(*all_in.shape, dtype=half_type),
            shape_of(*grad_weight.shape, dtype=half_type),
        ),
    )
    other_in = swap_half(sent_in)
    other_weight = swap_half(sent_weight)
    extra_in = local_call(
        stage_kernel, "stage_extra", (sent_in, extra_in), shape_of(*extra_in.shape), flops=LATE_START
    )
    damped_in = local_call(
        unpack_in_kernel,
        "unpack_in",
        (all_in, other_in),
        shape_of(*block, dtype=half_type),
        scratch=[pltpu.VMEM((packed_rows, TILE), half_type)],
    )
    inverse_in, right = local_call(
        invert_kernel,
        "invert",
        (damped_in, all_out, extra_in, extra_out),
        (shape_of(*block, dtype=half_type), shape_of(width, half, dtype=half_type)),
        scratch=[
            pltpu.VMEM(block, half_type),
            pltpu.VMEM(block, half_type),
            pltpu.VMEM(block, jnp.float32),
            pltpu.VMEM(block, jnp.float32),
        ],
        flops=8 * (ITERS - 1) * width * width * width,
    )
    return local_call(
        finish_kernel,
        "finish",
        (inverse_in, right, grad_weight, other_weight),
        shape_of(width, half, dtype=half_type),
        scratch=[pltpu.VMEM(block, half_type)],
        flops=3 * width * width * width,
    )


def solution(mesh):
    in_specs = (P("grp", "blk"), P("blk", "grp"), P("blk", "grp"))
    out_specs = P("blk", "grp")
    return jax.shard_map(shards, mesh=mesh, in_specs=in_specs, out_specs=out_specs, check_vma=False)
```

```python
import functools

import jax
import jax.numpy as jnp
from jax import lax
from jax.experimental import pallas as pl
from jax.experimental.pallas import tpu as pltpu
from jax.sharding import PartitionSpec as P

ITERS = 6
DAMP_ROOT = 0.1
TILE = 128
CORES = 2
CHUNKS = 2
RING = 4
EXTRA = 8
EXTRA_IN = 5
EXTRA_HALF = 16
LATE_START = 10**10
VMEM_LIMIT = 48 * 1024 * 1024
GRAM_LIMIT = 58 * 1024 * 1024


def tile_plan(count):
    off = [(i, j) for i in range(count) for j in range(i + 1, count)]
    pairs = [(i, i + 1) for i in range(0, count, 2)]
    return off, pairs


def tile_masks():
    rows = lax.broadcasted_iota(jnp.int32, (TILE, TILE), 0)
    cols = lax.broadcasted_iota(jnp.int32, (TILE, TILE), 1)
    return rows, cols


def gram_parts(data):
    half = data.shape[1] // 2
    low, high = data[:, :half], data[:, half:]
    return [
        lax.dot_general(left, right, (((0,), (0,)), ((), ())), preferred_element_type=jnp.float32)
        for left, right in ((low, low), (low, high), (high, high))
    ]


def pack_gram(quarters, store):
    per = quarters[0].shape[0] // TILE
    count = 2 * per

    def tile(i, j):
        part = quarters[i // per + j // per]
        r, c = (i % per) * TILE, (j % per) * TILE
        return part[r : r + TILE, c : c + TILE]

    off, pairs = tile_plan(count)
    rows, cols = tile_masks()
    for position, (i, j) in enumerate(off):
        store(position, tile(i, j))
    for position, (i, j) in enumerate(pairs):
        store(len(off) + position, jnp.where(cols > rows, tile(i, i), tile(j, j)))
    return jnp.concatenate(
        [
            jnp.sum(jnp.where(rows == cols, tile(i, i), 0.0), axis=0, keepdims=True)
            for i in range(count)
        ],
        axis=0,
    )


def unpack_block(fetch, out_ref):
    count = out_ref.shape[0] // TILE
    off, pairs = tile_plan(count)
    rows, cols = tile_masks()

    def put(i, j, value):
        out_ref[i * TILE : (i + 1) * TILE, j * TILE : (j + 1) * TILE] = value.astype(jnp.bfloat16)

    for position, (i, j) in enumerate(off):
        value = fetch(position).astype(jnp.float32)
        put(i, j, value)
        put(j, i, value.T)
    for position, (i, j) in enumerate(pairs):
        value = fetch(len(off) + position).astype(jnp.float32)
        other = value.T
        put(i, i, jnp.where(cols > rows, value, other))
        put(j, j, jnp.where(cols < rows, value, other))


def put_diagonal(diagonal, damping, out_ref):
    rows, cols = tile_masks()
    for i in range(out_ref.shape[0] // TILE):
        place = (slice(i * TILE, (i + 1) * TILE),) * 2
        damped = diagonal[i : i + 1, :] + damping
        tile = out_ref[place].astype(jnp.float32)
        out_ref[place] = jnp.where(rows == cols, damped, tile).astype(jnp.bfloat16)


def total_of(value):
    return jnp.sum(jnp.sum(value, axis=1, keepdims=True), axis=0, keepdims=True)


def gram_in_kernel(tokens, pieces, data_hbm, grads_hbm, out_ref, data_ref, grads_ref, sems):
    piece_rows = out_ref.shape[0] // pieces - EXTRA_IN
    per_tile = TILE // piece_rows
    scale = 1.0 / tokens
    rows = data_ref.shape[0] // CHUNKS
    copies = []
    for chunk in range(CHUNKS):
        place = pl.ds(chunk * rows, rows)
        copies.append(
            pltpu.make_async_copy(data_hbm.at[place], data_ref.at[place], sems.at[chunk])
        )
    copies.append(pltpu.make_async_copy(grads_hbm, grads_ref, sems.at[CHUNKS]))
    for copy in copies[CHUNKS:] + copies[:CHUNKS]:
        copy.start()
    copies[CHUNKS].wait()
    grads = grads_ref[...].astype(jnp.float32)
    energy = total_of(grads * grads) * scale
    for chunk in range(CHUNKS):
        copies[chunk].wait()
        part = gram_parts(data_ref[chunk * rows : (chunk + 1) * rows, :])
        quarters = part if chunk == 0 else [old + new for old, new in zip(quarters, part)]

    def store(position, value):
        for part in range(per_tile):
            start = (position * per_tile + part) * (piece_rows + EXTRA_IN)
            out_ref[start : start + piece_rows, :] = value[
                part * piece_rows : (part + 1) * piece_rows
            ]

    diagonal = pack_gram([scale * quarter for quarter in quarters], store)
    extra = jnp.concatenate([diagonal, jnp.broadcast_to(energy, (1, TILE))], axis=0)
    for piece in range(pieces):
        end = (piece + 1) * (piece_rows + EXTRA_IN)
        out_ref[end - EXTRA_IN : end, :] = extra


def gram_out_kernel(tokens, own_ref, other_ref, keep_ref, send_ref, data_ref, packed_ref):
    half = own_ref.shape[1]
    parity = lax.axis_index("grp") % 2
    core = lax.axis_index("blk") % CORES
    data_ref[:, pl.ds(pl.multiple_of(parity * half, half), half)] = own_ref[...]
    data_ref[:, pl.ds(pl.multiple_of((1 - parity) * half, half), half)] = other_ref[...]

    def store(position, value):
        packed_ref[position * TILE : (position + 1) * TILE, :] = value

    scale = 1.0 / tokens
    diagonal = pack_gram([scale * part for part in gram_parts(data_ref[...])], store)
    filler = jnp.zeros((EXTRA - diagonal.shape[0], TILE), jnp.float32)
    extra = jnp.concatenate([diagonal, filler], axis=0)
    share = keep_ref.shape[0] - EXTRA
    for ref, owner in ((keep_ref, core), (send_ref, 1 - core)):
        start = pl.multiple_of((parity * CORES + owner) * share, share)
        ref[:share, :] = packed_ref[pl.ds(start, share), :]
        ref[share:, :] = extra


def along_x():
    return lax.axis_index("blk") // (RING * CORES)


def fold_kernel(bit, left_ref, right_ref, keep_ref, give_ref):
    rows = keep_ref.shape[0] - EXTRA
    extra = left_ref[2 * rows :, :] + right_ref[2 * rows :, :]
    own = (along_x() >> bit) & 1
    for ref, owner in ((keep_ref, own), (give_ref, 1 - own)):
        place = pl.ds(pl.multiple_of(owner * rows, rows), rows)
        ref[:rows, :] = left_ref[place, :] + right_ref[place, :]
        ref[rows:, :] = extra


def stage_kernel(after_ref, value_ref, out_ref):
    out_ref[...] = value_ref[...]


def add_kernel(left_ref, right_ref, out_ref):
    out_ref[...] = left_ref[...] + right_ref[...]


def sum_pieces(ref, pieces):
    rows = ref.shape[0] // pieces
    total = ref[:rows, :]
    for piece in range(1, pieces):
        total = total + ref[piece * rows : (piece + 1) * rows, :]
    return total


def split_rows(value):
    high = value.astype(jnp.bfloat16).astype(jnp.float32)
    rest = value - high
    middle = rest.astype(jnp.bfloat16).astype(jnp.float32)
    return [high, middle, rest - middle]


def sum_in_kernel(pieces, got_ref, after_ref, send_ref, extra_ref):
    total = sum_pieces(got_ref, pieces)
    rows = send_ref.shape[1]
    rounded = total[:rows].astype(jnp.bfloat16)
    for piece in range(send_ref.shape[0]):
        send_ref[piece] = rounded
    filler = jnp.zeros((EXTRA - EXTRA_IN, TILE), jnp.float32)
    extra_ref[...] = jnp.concatenate([total[rows:], filler], axis=0)


def sum_x_kernel(count, left_ref, right_ref, extra_in_ref, out_ref):
    extra = extra_in_ref[...]
    total = left_ref[...] + right_ref[...]
    rows = total.shape[0] - EXTRA
    trace_in = jnp.broadcast_to(total_of(extra[:count]), (1, TILE))
    energy_out = extra[count : count + 1]
    filler = jnp.zeros((EXTRA - count - 2, TILE), jnp.float32)
    out_ref[...] = jnp.concatenate(
        [total[: rows + count], trace_in, energy_out, filler], axis=0
    )


def sum_y_kernel(count, left_ref, right_ref, send_ref, extra_ref):
    total = left_ref[...] + right_ref[...]
    rows = total.shape[0] - EXTRA
    extra = total[rows:]
    scalars = split_rows(extra[count : count + 1]) + split_rows(extra[count + 1 : count + 2])
    filler = jnp.zeros((EXTRA_HALF - len(scalars), TILE), jnp.float32)
    block = jnp.concatenate([total[:rows]] + scalars + [filler], axis=0).astype(jnp.bfloat16)
    for piece in range(send_ref.shape[0]):
        send_ref[piece] = block
    extra_ref[...] = extra


def stage_in_kernel(got_ref, weight_ref, sent_ref, sent_weight_ref):
    sent_ref[...] = got_ref[...]
    sent_weight_ref[...] = weight_ref[...]


def unpack_in_kernel(got_ref, other_ref, out_ref, packed_ref):
    rows = got_ref.shape[1]
    parity = lax.axis_index("grp") % 2
    for ref, place in ((got_ref, parity), (other_ref, 1 - parity)):
        for piece in range(ref.shape[0]):
            start = pl.multiple_of((2 * piece + place) * rows, rows)
            packed_ref[pl.ds(start, rows), :] = ref[piece]
    unpack_block(lambda position: packed_ref[position * TILE : (position + 1) * TILE, :], out_ref)


def invert_kernel(
    damped_in_ref,
    got_out_ref,
    extra_in_ref,
    extra_out_ref,
    inverse_ref,
    right_ref,
    full_in_ref,
    damped_out_ref,
    iterate_in_ref,
    iterate_out_ref,
):
    width = damped_in_ref.shape[0]
    count = width // TILE
    half = right_ref.shape[1]
    parity = lax.axis_index("grp") % 2
    pieces, rows_out = got_out_ref.shape[0], got_out_ref.shape[1] - EXTRA_HALF
    own_column = pl.ds(pl.multiple_of(parity * half, half), half)

    scalars = jnp.zeros((EXTRA_HALF, TILE), jnp.float32)
    for piece in range(pieces // 2):
        scalars = scalars + got_out_ref[piece, rows_out:, :].astype(jnp.float32)
    sum_in = scalars[0:1] + scalars[1:2] + scalars[2:3]
    sum_out = scalars[3:4] + scalars[4:5] + scalars[5:6]
    owners = lax.axis_size("blk")
    blocks_out = lax.axis_size("grp") // 2
    pi_ratio = jnp.sqrt((sum_in / (owners * width)) / (sum_out / (blocks_out * width)))
    damping_in = DAMP_ROOT * pi_ratio
    damping_out = DAMP_ROOT / pi_ratio
    diagonal_in = extra_in_ref[:count, :]
    diagonal_out = extra_out_ref[:count, :]
    scale_in = 1.0 / (total_of(diagonal_in) + width * damping_in)
    scale_out = 1.0 / (total_of(diagonal_out) + width * damping_out)

    full_in_ref[...] = damped_in_ref[...]
    put_diagonal(diagonal_in, damping_in, full_in_ref)
    def fetch_out(position):
        per_tile = TILE // rows_out
        pair = position // RING
        core, first = position % RING // CORES, position % CORES * per_tile
        return jnp.concatenate(
            [
                got_out_ref[(pair * RING + first + part) * CORES + core, :rows_out, :]
                for part in range(per_tile)
            ],
            axis=0,
        )

    unpack_block(fetch_out, damped_out_ref)
    put_diagonal(diagonal_out, damping_out, damped_out_ref)

    chains = (
        (full_in_ref, iterate_in_ref, scale_in),
        (damped_out_ref, iterate_out_ref, scale_out),
    )
    rows, cols = tile_masks()
    for damped, iterate, scale in chains:
        factor = scale.astype(jnp.bfloat16).astype(jnp.float32)
        twice = jnp.where(rows == cols, 2.0 * scale, 0.0)
        for i in range(count):
            for j in range(count):
                place = (slice(i * TILE, (i + 1) * TILE), slice(j * TILE, (j + 1) * TILE))
                product = (damped[place].astype(jnp.float32) * factor).astype(jnp.bfloat16)
                moved = product.astype(jnp.float32) * factor
                iterate[place] = (twice - moved) if i == j else -moved

    for _ in range(ITERS - 1):
        currents = [iterate[...].astype(jnp.bfloat16) for _, iterate, _ in chains]
        products = [
            jnp.dot(damped[...], current, preferred_element_type=jnp.float32).astype(jnp.bfloat16)
            for (damped, _, _), current in zip(chains, currents)
        ]
        for (_, iterate, _), product, current in zip(chains, products, currents):
            iterate[...] = 2.0 * iterate[...] - jnp.dot(
                product, current, preferred_element_type=jnp.float32
            )
    inverse_ref[...] = iterate_in_ref[...].astype(jnp.bfloat16)
    right_ref[...] = iterate_out_ref[:, own_column].astype(jnp.bfloat16)


def finish_kernel(inverse_ref, right_ref, weight_ref, other_weight_ref, result_ref, left_ref):
    half = weight_ref.shape[1]
    parity = lax.axis_index("grp") % 2
    for ref, place in ((weight_ref, parity), (other_weight_ref, 1 - parity)):
        left_ref[:, pl.ds(pl.multiple_of(place * half, half), half)] = jnp.dot(
            inverse_ref[...], ref[...], preferred_element_type=jnp.float32
        ).astype(jnp.bfloat16)
    result_ref[...] = jnp.dot(
        left_ref[...], right_ref[...], preferred_element_type=jnp.float32
    ).astype(jnp.bfloat16)


VMEM_SPEC = pl.BlockSpec(memory_space=pltpu.VMEM)


def local_call(kernel, name, operands, outs, scratch=(), flops=0, space=pltpu.VMEM, limit=VMEM_LIMIT):
    multiple = isinstance(outs, tuple)
    listed = outs if multiple else (outs,)
    moved = sum(a.size * a.dtype.itemsize for a in operands + tuple(listed))
    return pl.pallas_call(
        kernel,
        out_shape=outs,
        in_specs=[pl.BlockSpec(memory_space=space)] * len(operands),
        out_specs=tuple([VMEM_SPEC] * len(listed)) if multiple else VMEM_SPEC,
        scratch_shapes=list(scratch),
        compiler_params=pltpu.CompilerParams(vmem_limit_bytes=limit),
        cost_estimate=pl.CostEstimate(flops=flops, bytes_accessed=moved, transcendentals=0),
        name=name,
    )(*operands)


def shape_of(*dims, dtype=jnp.float32):
    return jax.ShapeDtypeStruct(dims, dtype)


def exchange(value, axis, groups=None):
    return lax.all_to_all(value, axis, 0, 0, tiled=True, axis_index_groups=groups)


def swap_core(value):
    pairs = [(place, place ^ 1) for place in range(lax.axis_size("blk"))]
    return lax.ppermute(value, "blk", pairs)


def swap_along(value, stride, step):
    pairs = [(place, place ^ (stride * step)) for place in range(lax.axis_size("blk"))]
    return lax.ppermute(value, "blk", pairs)


def swap_half(value):
    pairs = [(place, place ^ 1) for place in range(lax.axis_size("grp"))]
    return lax.ppermute(value, "grp", pairs)


def shards(activations, output_grads, grad_weight):
    groups = lax.axis_size("grp")
    width = grad_weight.shape[0]
    half = grad_weight.shape[1]
    count = width // TILE
    packed_rows = width * width // (2 * TILE)
    total_tokens = activations.shape[0] * groups
    in_rows = packed_rows // groups
    share_rows = packed_rows // (2 * CORES)
    piece_rows = share_rows // RING
    y_stride, x_stride = CORES, CORES * RING
    half_type = jnp.bfloat16

    other_grads = swap_half(output_grads)
    send_in = local_call(
        functools.partial(gram_in_kernel, total_tokens, groups),
        "gram_in",
        (activations, output_grads),
        shape_of(groups * (in_rows + EXTRA_IN), TILE),
        scratch=[
            pltpu.VMEM(activations.shape, half_type),
            pltpu.VMEM(output_grads.shape, half_type),
            pltpu.SemaphoreType.DMA((CHUNKS + 1,)),
        ],
        flops=2 * activations.shape[0] * width * width,
        space=pltpu.HBM,
        limit=GRAM_LIMIT,
    )
    got_in = exchange(send_in.reshape(groups, -1, 1, TILE), "grp").reshape(-1, TILE)

    keep, give = local_call(
        functools.partial(gram_out_kernel, total_tokens),
        "gram_out",
        (output_grads, other_grads),
        (shape_of(share_rows + EXTRA, TILE),) * 2,
        scratch=[
            pltpu.VMEM((output_grads.shape[0], width), half_type),
            pltpu.VMEM((packed_rows, TILE), jnp.float32),
        ],
        flops=LATE_START * 3,
    )
    folds = (
        ("fold_cores", 1, share_rows // 2, swap_core),
        ("fold_x", 0, piece_rows, lambda value: swap_along(value, x_stride, 3)),
    )
    for name, bit, rows, swap in folds:
        keep, give = local_call(
            functools.partial(fold_kernel, bit),
            name,
            (keep, swap(give)),
            (shape_of(rows + EXTRA, TILE),) * 2,
        )
    to_all_in, extra_in = local_call(
        functools.partial(sum_in_kernel, groups),
        "sum_in",
        (got_in, keep),
        (shape_of(groups // 2, in_rows, TILE, dtype=half_type), shape_of(EXTRA, TILE)),
    )
    same_half = [list(range(parity, groups, 2)) for parity in range(2)]
    all_in = exchange(to_all_in, "grp", same_half)
    part_y = local_call(
        functools.partial(sum_x_kernel, count),
        "sum_x",
        (keep, swap_along(give, x_stride, 1), extra_in),
        shape_of(piece_rows + EXTRA, TILE),
        flops=LATE_START,
    )
    part_y = local_call(
        add_kernel,
        "add_y",
        (part_y, swap_along(part_y, y_stride, 1)),
        shape_of(*part_y.shape),
        flops=LATE_START,
    )
    to_all_out, extra_out = local_call(
        functools.partial(sum_y_kernel, count),
        "sum_y",
        (part_y, swap_along(part_y, y_stride, 3)),
        (
            shape_of(2 * RING * CORES, piece_rows + EXTRA_HALF, TILE, dtype=half_type),
            shape_of(EXTRA, TILE),
        ),
    )
    owners = lax.axis_size("blk")
    same_plane = [
        [
            (2 * z + parity) * owners + x * x_stride + y * y_stride + core
            for parity in range(2)
            for x in range(RING)
            for core in range(CORES)
        ]
        for z in range(groups // 2)
        for y in range(RING)
    ]
    all_out = exchange(to_all_out, ("grp", "blk"), same_plane)

    block = (width, width)
    all_in, extra_out = lax.optimization_barrier((all_in, extra_out))
    sent_in, sent_weight = local_call(
        stage_in_kernel,
        "stage_in",
        (all_in, grad_weight),
        (
            shape_of(*all_in.shape, dtype=half_type),
            shape_of(*grad_weight.shape, dtype=half_type),
        ),
    )
    other_in = swap_half(sent_in)
    other_weight = swap_half(sent_weight)
    extra_in = local_call(
        stage_kernel, "stage_extra", (sent_in, extra_in), shape_of(*extra_in.shape), flops=LATE_START
    )
    damped_in = local_call(
        unpack_in_kernel,
        "unpack_in",
        (all_in, other_in),
        shape_of(*block, dtype=half_type),
        scratch=[pltpu.VMEM((packed_rows, TILE), half_type)],
    )
    inverse_in, right = local_call(
        invert_kernel,
        "invert",
        (damped_in, all_out, extra_in, extra_out),
        (shape_of(*block, dtype=half_type), shape_of(width, half, dtype=half_type)),
        scratch=[
            pltpu.VMEM(block, half_type),
            pltpu.VMEM(block, half_type),
            pltpu.VMEM(block, jnp.float32),
            pltpu.VMEM(block, jnp.float32),
        ],
        flops=8 * (ITERS - 1) * width * width * width,
    )
    return local_call(
        finish_kernel,
        "finish",
        (inverse_in, right, grad_weight, other_weight),
        shape_of(width, half, dtype=half_type),
        scratch=[pltpu.VMEM(block, half_type)],
        flops=3 * width * width * width,
    )


def solution(mesh):
    in_specs = (P("grp", "blk"), P("blk", "grp"), P("blk", "grp"))
    out_specs = P("blk", "grp")
    return jax.shard_map(shards, mesh=mesh, in_specs=in_specs, out_specs=out_specs, check_vma=False)
```

```python
import functools

import jax
import jax.numpy as jnp
from jax import lax
from jax.experimental import pallas as pl
from jax.experimental.pallas import tpu as pltpu
from jax.sharding import PartitionSpec as P

ITERS = 6
DAMP_ROOT = 0.1
TILE = 128
CORES = 2
CHUNKS = 2
RING = 4
EXTRA = 8
EXTRA_HALF = 16
LATE_START = 10**10
VMEM_LIMIT = 48 * 1024 * 1024
GRAM_LIMIT = 58 * 1024 * 1024


def tile_plan(count):
    off = [(i, j) for i in range(count) for j in range(i + 1, count)]
    pairs = [(i, i + 1) for i in range(0, count, 2)]
    return off, pairs


def tile_masks():
    rows = lax.broadcasted_iota(jnp.int32, (TILE, TILE), 0)
    cols = lax.broadcasted_iota(jnp.int32, (TILE, TILE), 1)
    return rows, cols


def gram_parts(data):
    half = data.shape[1] // 2
    low, high = data[:, :half], data[:, half:]
    return [
        lax.dot_general(left, right, (((0,), (0,)), ((), ())), preferred_element_type=jnp.float32)
        for left, right in ((low, low), (low, high), (high, high))
    ]


def pack_gram(quarters, store):
    per = quarters[0].shape[0] // TILE
    count = 2 * per

    def tile(i, j):
        part = quarters[i // per + j // per]
        r, c = (i % per) * TILE, (j % per) * TILE
        return part[r : r + TILE, c : c + TILE]

    off, pairs = tile_plan(count)
    rows, cols = tile_masks()
    for position, (i, j) in enumerate(off):
        store(position, tile(i, j))
    for position, (i, j) in enumerate(pairs):
        store(len(off) + position, jnp.where(cols > rows, tile(i, i), tile(j, j)))
    return jnp.concatenate(
        [
            jnp.sum(jnp.where(rows == cols, tile(i, i), 0.0), axis=0, keepdims=True)
            for i in range(count)
        ],
        axis=0,
    )


def unpack_block(fetch, out_ref):
    count = out_ref.shape[0] // TILE
    off, pairs = tile_plan(count)
    rows, cols = tile_masks()

    def put(i, j, value):
        out_ref[i * TILE : (i + 1) * TILE, j * TILE : (j + 1) * TILE] = value.astype(jnp.bfloat16)

    for position, (i, j) in enumerate(off):
        value = fetch(position).astype(jnp.float32)
        put(i, j, value)
        put(j, i, value.T)
    for position, (i, j) in enumerate(pairs):
        value = fetch(len(off) + position).astype(jnp.float32)
        other = value.T
        put(i, i, jnp.where(cols > rows, value, other))
        put(j, j, jnp.where(cols < rows, value, other))


def put_diagonal(diagonal, damping, out_ref):
    rows, cols = tile_masks()
    for i in range(out_ref.shape[0] // TILE):
        place = (slice(i * TILE, (i + 1) * TILE),) * 2
        damped = diagonal[i : i + 1, :] + damping
        tile = out_ref[place].astype(jnp.float32)
        out_ref[place] = jnp.where(rows == cols, damped, tile).astype(jnp.bfloat16)


def total_of(value):
    return jnp.sum(jnp.sum(value, axis=1, keepdims=True), axis=0, keepdims=True)


def gram_in_kernel(tokens, data_hbm, grads_hbm, out_ref, data_ref, grads_ref, sems):
    pieces, piece_rows = out_ref.shape[0], out_ref.shape[1] - EXTRA
    per_tile = TILE // piece_rows
    scale = 1.0 / tokens
    rows = data_ref.shape[0] // CHUNKS
    copies = []
    for chunk in range(CHUNKS):
        place = pl.ds(chunk * rows, rows)
        copies.append(
            pltpu.make_async_copy(data_hbm.at[place], data_ref.at[place], sems.at[chunk])
        )
    copies.append(pltpu.make_async_copy(grads_hbm, grads_ref, sems.at[CHUNKS]))
    for copy in copies[CHUNKS:] + copies[:CHUNKS]:
        copy.start()
    copies[CHUNKS].wait()
    grads = grads_ref[...].astype(jnp.float32)
    energy = total_of(grads * grads) * scale
    for chunk in range(CHUNKS):
        copies[chunk].wait()
        part = gram_parts(data_ref[chunk * rows : (chunk + 1) * rows, :])
        quarters = part if chunk == 0 else [old + new for old, new in zip(quarters, part)]

    def store(position, value):
        for part in range(per_tile):
            out_ref[position * per_tile + part, :piece_rows, :] = value[
                part * piece_rows : (part + 1) * piece_rows
            ]

    diagonal = pack_gram([scale * quarter for quarter in quarters], store)
    filler = jnp.zeros((EXTRA - diagonal.shape[0] - 1, TILE), jnp.float32)
    extra = jnp.concatenate(
        [diagonal, jnp.broadcast_to(energy, (1, TILE)), filler], axis=0
    )
    for piece in range(pieces):
        out_ref[piece, piece_rows:, :] = extra


def gram_out_kernel(tokens, own_ref, other_ref, keep_ref, send_ref, data_ref, packed_ref):
    half = own_ref.shape[1]
    parity = lax.axis_index("grp") % 2
    core = lax.axis_index("blk") % CORES
    data_ref[:, pl.ds(pl.multiple_of(parity * half, half), half)] = own_ref[...]
    data_ref[:, pl.ds(pl.multiple_of((1 - parity) * half, half), half)] = other_ref[...]

    def store(position, value):
        packed_ref[position * TILE : (position + 1) * TILE, :] = value

    scale = 1.0 / tokens
    diagonal = pack_gram([scale * part for part in gram_parts(data_ref[...])], store)
    filler = jnp.zeros((EXTRA - diagonal.shape[0], TILE), jnp.float32)
    extra = jnp.concatenate([diagonal, filler], axis=0)
    share = keep_ref.shape[0] - EXTRA
    for ref, owner in ((keep_ref, core), (send_ref, 1 - core)):
        start = pl.multiple_of((parity * CORES + owner) * share, share)
        ref[:share, :] = packed_ref[pl.ds(start, share), :]
        ref[share:, :] = extra


def along_x():
    return lax.axis_index("blk") // (RING * CORES)


def fold_kernel(bit, left_ref, right_ref, keep_ref, give_ref):
    rows = keep_ref.shape[0] - EXTRA
    extra = left_ref[2 * rows :, :] + right_ref[2 * rows :, :]
    own = (along_x() >> bit) & 1
    for ref, owner in ((keep_ref, own), (give_ref, 1 - own)):
        place = pl.ds(pl.multiple_of(owner * rows, rows), rows)
        ref[:rows, :] = left_ref[place, :] + right_ref[place, :]
        ref[rows:, :] = extra


def stage_kernel(after_ref, value_ref, out_ref):
    out_ref[...] = value_ref[...]


def add_kernel(left_ref, right_ref, out_ref):
    out_ref[...] = left_ref[...] + right_ref[...]


def sum_pieces(ref):
    total = ref[0]
    for piece in range(1, ref.shape[0]):
        total = total + ref[piece]
    return total


def split_rows(value):
    high = value.astype(jnp.bfloat16).astype(jnp.float32)
    rest = value - high
    middle = rest.astype(jnp.bfloat16).astype(jnp.float32)
    return [high, middle, rest - middle]


def sum_in_kernel(got_ref, after_ref, send_ref, extra_ref):
    total = sum_pieces(got_ref)
    rows = send_ref.shape[1]
    rounded = total[:rows].astype(jnp.bfloat16)
    for piece in range(send_ref.shape[0]):
        send_ref[piece] = rounded
    extra_ref[...] = total[rows:]


def sum_x_kernel(count, left_ref, right_ref, extra_in_ref, out_ref):
    extra = extra_in_ref[...]
    total = left_ref[...] + right_ref[...]
    rows = total.shape[0] - EXTRA
    trace_in = jnp.broadcast_to(total_of(extra[:count]), (1, TILE))
    energy_out = extra[count : count + 1]
    filler = jnp.zeros((EXTRA - count - 2, TILE), jnp.float32)
    out_ref[...] = jnp.concatenate(
        [total[: rows + count], trace_in, energy_out, filler], axis=0
    )


def sum_y_kernel(count, left_ref, right_ref, send_ref, extra_ref):
    total = left_ref[...] + right_ref[...]
    rows = total.shape[0] - EXTRA
    extra = total[rows:]
    scalars = split_rows(extra[count : count + 1]) + split_rows(extra[count + 1 : count + 2])
    filler = jnp.zeros((EXTRA_HALF - len(scalars), TILE), jnp.float32)
    block = jnp.concatenate([total[:rows]] + scalars + [filler], axis=0).astype(jnp.bfloat16)
    for piece in range(send_ref.shape[0]):
        send_ref[piece] = block
    extra_ref[...] = extra


def stage_in_kernel(got_ref, weight_ref, sent_ref, sent_weight_ref):
    sent_ref[...] = got_ref[...]
    sent_weight_ref[...] = weight_ref[...]


def unpack_in_kernel(got_ref, other_ref, out_ref, packed_ref):
    rows = got_ref.shape[1]
    parity = lax.axis_index("grp") % 2
    for ref, place in ((got_ref, parity), (other_ref, 1 - parity)):
        for piece in range(ref.shape[0]):
            start = pl.multiple_of((2 * piece + place) * rows, rows)
            packed_ref[pl.ds(start, rows), :] = ref[piece]
    unpack_block(lambda position: packed_ref[position * TILE : (position + 1) * TILE, :], out_ref)


def invert_kernel(
    damped_in_ref,
    got_out_ref,
    extra_in_ref,
    extra_out_ref,
    inverse_ref,
    right_ref,
    full_in_ref,
    damped_out_ref,
    iterate_in_ref,
    iterate_out_ref,
):
    width = damped_in_ref.shape[0]
    count = width // TILE
    half = right_ref.shape[1]
    parity = lax.axis_index("grp") % 2
    pieces, rows_out = got_out_ref.shape[0], got_out_ref.shape[1] - EXTRA_HALF
    own_column = pl.ds(pl.multiple_of(parity * half, half), half)

    scalars = jnp.zeros((EXTRA_HALF, TILE), jnp.float32)
    for piece in range(0, pieces, 2):
        scalars = scalars + got_out_ref[piece, rows_out:, :].astype(jnp.float32)
    sum_in = scalars[0:1] + scalars[1:2] + scalars[2:3]
    sum_out = scalars[3:4] + scalars[4:5] + scalars[5:6]
    owners = lax.axis_size("blk")
    blocks_out = lax.axis_size("grp") // 2
    pi_ratio = jnp.sqrt((sum_in / (owners * width)) / (sum_out / (blocks_out * width)))
    damping_in = DAMP_ROOT * pi_ratio
    damping_out = DAMP_ROOT / pi_ratio
    diagonal_in = extra_in_ref[:count, :]
    diagonal_out = extra_out_ref[:count, :]
    scale_in = 1.0 / (total_of(diagonal_in) + width * damping_in)
    scale_out = 1.0 / (total_of(diagonal_out) + width * damping_out)

    full_in_ref[...] = damped_in_ref[...]
    put_diagonal(diagonal_in, damping_in, full_in_ref)
    def fetch_out(position):
        per_tile = TILE // rows_out
        pair = position // RING
        core, first = position % RING // CORES, position % CORES * per_tile
        return jnp.concatenate(
            [
                got_out_ref[((first + part) * CORES + core) * 2 + pair, :rows_out, :]
                for part in range(per_tile)
            ],
            axis=0,
        )

    unpack_block(fetch_out, damped_out_ref)
    put_diagonal(diagonal_out, damping_out, damped_out_ref)

    chains = (
        (full_in_ref, iterate_in_ref, scale_in),
        (damped_out_ref, iterate_out_ref, scale_out),
    )
    rows, cols = tile_masks()
    for damped, iterate, scale in chains:
        factor = scale.astype(jnp.bfloat16).astype(jnp.float32)
        twice = jnp.where(rows == cols, 2.0 * scale, 0.0)
        for i in range(count):
            for j in range(count):
                place = (slice(i * TILE, (i + 1) * TILE), slice(j * TILE, (j + 1) * TILE))
                product = (damped[place].astype(jnp.float32) * factor).astype(jnp.bfloat16)
                moved = product.astype(jnp.float32) * factor
                iterate[place] = (twice - moved) if i == j else -moved

    for _ in range(ITERS - 1):
        currents = [iterate[...].astype(jnp.bfloat16) for _, iterate, _ in chains]
        products = [
            jnp.dot(damped[...], current, preferred_element_type=jnp.float32).astype(jnp.bfloat16)
            for (damped, _, _), current in zip(chains, currents)
        ]
        for (_, iterate, _), product, current in zip(chains, products, currents):
            iterate[...] = 2.0 * iterate[...] - jnp.dot(
                product, current, preferred_element_type=jnp.float32
            )
    inverse_ref[...] = iterate_in_ref[...].astype(jnp.bfloat16)
    right_ref[...] = iterate_out_ref[:, own_column].astype(jnp.bfloat16)


def finish_kernel(inverse_ref, right_ref, weight_ref, other_weight_ref, result_ref, left_ref):
    half = weight_ref.shape[1]
    parity = lax.axis_index("grp") % 2
    for ref, place in ((weight_ref, parity), (other_weight_ref, 1 - parity)):
        left_ref[:, pl.ds(pl.multiple_of(place * half, half), half)] = jnp.dot(
            inverse_ref[...], ref[...], preferred_element_type=jnp.float32
        ).astype(jnp.bfloat16)
    result_ref[...] = jnp.dot(
        left_ref[...], right_ref[...], preferred_element_type=jnp.float32
    ).astype(jnp.bfloat16)


VMEM_SPEC = pl.BlockSpec(memory_space=pltpu.VMEM)


def local_call(kernel, name, operands, outs, scratch=(), flops=0, space=pltpu.VMEM, limit=VMEM_LIMIT):
    multiple = isinstance(outs, tuple)
    listed = outs if multiple else (outs,)
    moved = sum(a.size * a.dtype.itemsize for a in operands + tuple(listed))
    return pl.pallas_call(
        kernel,
        out_shape=outs,
        in_specs=[pl.BlockSpec(memory_space=space)] * len(operands),
        out_specs=tuple([VMEM_SPEC] * len(listed)) if multiple else VMEM_SPEC,
        scratch_shapes=list(scratch),
        compiler_params=pltpu.CompilerParams(vmem_limit_bytes=limit),
        cost_estimate=pl.CostEstimate(flops=flops, bytes_accessed=moved, transcendentals=0),
        name=name,
    )(*operands)


def shape_of(*dims, dtype=jnp.float32):
    return jax.ShapeDtypeStruct(dims, dtype)


def exchange(value, axis, groups=None):
    return lax.all_to_all(value, axis, 0, 0, tiled=True, axis_index_groups=groups)


def swap_core(value):
    pairs = [(place, place ^ 1) for place in range(lax.axis_size("blk"))]
    return lax.ppermute(value, "blk", pairs)


def swap_along(value, stride, step):
    pairs = [(place, place ^ (stride * step)) for place in range(lax.axis_size("blk"))]
    return lax.ppermute(value, "blk", pairs)


def swap_half(value):
    pairs = [(place, place ^ 1) for place in range(lax.axis_size("grp"))]
    return lax.ppermute(value, "grp", pairs)


def shards(activations, output_grads, grad_weight):
    groups = lax.axis_size("grp")
    width = grad_weight.shape[0]
    half = grad_weight.shape[1]
    count = width // TILE
    packed_rows = width * width // (2 * TILE)
    total_tokens = activations.shape[0] * groups
    in_rows = packed_rows // groups
    share_rows = packed_rows // (2 * CORES)
    piece_rows = share_rows // RING
    y_stride, x_stride = CORES, CORES * RING
    half_type = jnp.bfloat16

    other_grads = swap_half(output_grads)
    send_in = local_call(
        functools.partial(gram_in_kernel, total_tokens),
        "gram_in",
        (activations, output_grads),
        shape_of(groups, in_rows + EXTRA, TILE),
        scratch=[
            pltpu.VMEM(activations.shape, half_type),
            pltpu.VMEM(output_grads.shape, half_type),
            pltpu.SemaphoreType.DMA((CHUNKS + 1,)),
        ],
        flops=2 * activations.shape[0] * width * width,
        space=pltpu.HBM,
        limit=GRAM_LIMIT,
    )
    got_in = exchange(send_in, "grp")

    keep, give = local_call(
        functools.partial(gram_out_kernel, total_tokens),
        "gram_out",
        (output_grads, other_grads),
        (shape_of(share_rows + EXTRA, TILE),) * 2,
        scratch=[
            pltpu.VMEM((output_grads.shape[0], width), half_type),
            pltpu.VMEM((packed_rows, TILE), jnp.float32),
        ],
        flops=LATE_START * 3,
    )
    folds = (
        ("fold_cores", 1, share_rows // 2, swap_core),
        ("fold_x", 0, piece_rows, lambda value: swap_along(value, x_stride, 3)),
    )
    for name, bit, rows, swap in folds:
        keep, give = local_call(
            functools.partial(fold_kernel, bit),
            name,
            (keep, swap(give)),
            (shape_of(rows + EXTRA, TILE),) * 2,
        )
    to_all_in, extra_in = local_call(
        sum_in_kernel,
        "sum_in",
        (got_in, keep),
        (shape_of(groups // 2, in_rows, TILE, dtype=half_type), shape_of(EXTRA, TILE)),
    )
    same_half = [list(range(parity, groups, 2)) for parity in range(2)]
    all_in = exchange(to_all_in, "grp", same_half)
    part_y = local_call(
        functools.partial(sum_x_kernel, count),
        "sum_x",
        (keep, swap_along(give, x_stride, 1), extra_in),
        shape_of(piece_rows + EXTRA, TILE),
        flops=LATE_START,
    )
    part_y = local_call(
        add_kernel,
        "add_y",
        (part_y, swap_along(part_y, y_stride, 1)),
        shape_of(*part_y.shape),
        flops=LATE_START,
    )
    to_all_out, extra_out = local_call(
        functools.partial(sum_y_kernel, count),
        "sum_y",
        (part_y, swap_along(part_y, y_stride, 3)),
        (
            shape_of(2 * RING * CORES, piece_rows + EXTRA_HALF, TILE, dtype=half_type),
            shape_of(EXTRA, TILE),
        ),
    )
    owners = lax.axis_size("blk")
    same_plane = [
        [
            (2 * z + parity) * owners + x * x_stride + y * y_stride + core
            for x in range(RING)
            for core in range(CORES)
            for parity in range(2)
        ]
        for z in range(groups // 2)
        for y in range(RING)
    ]
    all_out = exchange(to_all_out, ("grp", "blk"), same_plane)

    block = (width, width)
    all_in, extra_out = lax.optimization_barrier((all_in, extra_out))
    sent_in, sent_weight = local_call(
        stage_in_kernel,
        "stage_in",
        (all_in, grad_weight),
        (
            shape_of(*all_in.shape, dtype=half_type),
            shape_of(*grad_weight.shape, dtype=half_type),
        ),
    )
    other_in = swap_half(sent_in)
    other_weight = swap_half(sent_weight)
    extra_in = local_call(
        stage_kernel, "stage_extra", (sent_in, extra_in), shape_of(*extra_in.shape), flops=LATE_START
    )
    damped_in = local_call(
        unpack_in_kernel,
        "unpack_in",
        (all_in, other_in),
        shape_of(*block, dtype=half_type),
        scratch=[pltpu.VMEM((packed_rows, TILE), half_type)],
    )
    inverse_in, right = local_call(
        invert_kernel,
        "invert",
        (damped_in, all_out, extra_in, extra_out),
        (shape_of(*block, dtype=half_type), shape_of(width, half, dtype=half_type)),
        scratch=[
            pltpu.VMEM(block, half_type),
            pltpu.VMEM(block, half_type),
            pltpu.VMEM(block, jnp.float32),
            pltpu.VMEM(block, jnp.float32),
        ],
        flops=8 * (ITERS - 1) * width * width * width,
    )
    return local_call(
        finish_kernel,
        "finish",
        (inverse_in, right, grad_weight, other_weight),
        shape_of(width, half, dtype=half_type),
        scratch=[pltpu.VMEM(block, half_type)],
        flops=3 * width * width * width,
    )


def solution(mesh):
    in_specs = (P("grp", "blk"), P("blk", "grp"), P("blk", "grp"))
    out_specs = P("blk", "grp")
    return jax.shard_map(shards, mesh=mesh, in_specs=in_specs, out_specs=out_specs, check_vma=False)
```
